128 devices in a mesh: rep: 16 (over z, y_hi, core), shard: 8 (over x, y_lo).
Axes of the slice: x: 4, y: 4 (y_hi: 2, y_lo: 2; y = y_hi * 2 + y_lo), z: 4, core: 2. Of those that a mesh axis runs over, the one named last changes fastest.
Arguments:
- hidden: bfloat16 [16384, 1024], P(('rep', 'shard')), may hold values from -6 to 6
- w_in: bfloat16 [1024, 3072], P('shard'), may hold values from -0.1875 to 0.1875
- conv_taps: float32 [3, 1024], replicated, may hold values from -3 to 3
- w_out: bfloat16 [1024, 1024], P('shard'), may hold values from -0.1875 to 0.1875
- gain_mix: float32 [1024], replicated, may hold values from 0.1 to 1.9
- gain_ffn: float32 [1024], replicated, may hold values from 0.1 to 1.9
- w_gate: bfloat16 [1024, 4608], P('shard'), may hold values from -0.1875 to 0.1875
- w_up: bfloat16 [1024, 4608], P('shard'), may hold values from -0.1875 to 0.1875
- w_down: bfloat16 [1024, 4608], P('shard'), may hold values from -0.09375 to 0.09375
- cotangent: bfloat16 [16384, 1024], P(('rep', 'shard')), may hold values from -6 to 6
- counts: int32 [16, 8], P('rep'), may hold values from 64 to 128, as said below
- lengths: int32 [16, 4], P('rep'), may hold values from 1 to 765, as said below
Outputs:
- result: float32 [16384, 1024], P(('rep', 'shard'))
- grad_hidden: float32 [16384, 1024], P(('rep', 'shard'))
- grad_w_in: float32 [1024, 3072], P('shard')
- grad_conv_taps: float32 [3, 1024], replicated
- grad_w_out: float32 [1024, 1024], P('shard')
- grad_gain_mix: float32 [1024], replicated
- grad_gain_ffn: float32 [1024], replicated
- grad_w_gate: float32 [1024, 4608], P('shard')
- grad_w_up: float32 [1024, 4608], P('shard')
- grad_w_down: float32 [1024, 4608], P('shard')
The draws below stay inside these ranges and needn't reach their ends.
Inputs may be any that keep to these rules, and one draw needn't show every extreme that they name: counts[r, s] is the number of live rows at the start of the 128 rows of device s of replica group r; the counts of devices 2k and 2k+1 of a group sum to 192, so a group has 768 live rows. Positive lengths of a group's sequences in order, summing to 768.
All inputs are finite; a program needn't handle non-finite values.
Results may differ from the reference program's by a relative error of at most 0.023.
Values may be sent and summed in bfloat16 or wider, within the bound.
No kernel may reach another device: no remote copies, remote signals or barrier semaphores. Data moves between devices by JAX's collectives and lax.ppermute only.
A program may use at most 256 MiB of HBM per device.

```python
from functools import partial
import jax
import jax.numpy as jnp
from jax import lax

D = 1024
FF = 4608
TOK_DEV = 128
GROUP_LIVE = 768
TOKENS = 16384
N_REP = 16
N_SHARD = 8


def draw_counts(key, part):
    key = jax.random.fold_in(key, 11)
    key_extra, key_pick = jax.random.split(key)
    half = TOK_DEV // 2
    pairs = N_SHARD // 2
    extra = jax.random.randint(key_extra, (N_REP, pairs), 0, half + 1)
    chosen = jax.random.randint(key_pick, (N_REP, 1), 0, pairs)
    extra = jnp.where(jnp.arange(pairs)[None, :] == chosen, 0, extra)
    lower = half + extra
    upper = TOK_DEV - extra
    return jnp.stack([lower, upper], axis=2).reshape(N_REP, N_SHARD).astype(jnp.int32)


def draw_lengths(key, part):
    key = jax.random.fold_in(key, 23)
    key_head, key_one, key_two, key_group = jax.random.split(key, 4)
    quarter = TOK_DEV // 4
    head = jax.random.randint(key_head, (N_REP, 1), 1, quarter + 1)
    tail_one = jax.random.randint(key_one, (N_REP, 1), 1, quarter // 2 + 1)
    tail_two = jax.random.randint(key_two, (N_REP, 1), 1, quarter // 2 + 1)
    picked = jax.random.randint(key_group, (), 0, N_REP)
    forced = (jnp.arange(N_REP) == picked)[:, None]
    head = jnp.where(forced, 1, head)
    tail_one = jnp.where(forced, 1, tail_one)
    tail_two = jnp.where(forced, 1, tail_two)
    longest = GROUP_LIVE - head - tail_one - tail_two
    return jnp.concatenate([head, longest, tail_one, tail_two], axis=1).astype(jnp.int32)


def level_of(rng, dims, shards, low, largest):
    level = 1.0
    for position, parts in shards:
        heights = jax.random.uniform(jax.random.fold_in(jax.random.fold_in(rng, 6), position), (parts,), jnp.float32, low / len(shards), largest / len(shards))
        level = level * jnp.repeat(jnp.exp(heights), dims[position] // parts).reshape((-1,) + (1,) * (len(dims) - 1 - position))
    return level


def normal_values(key, dims, deviation, reach, cuts=(), held_as=jnp.bfloat16):
    loudness = level_of(key, dims, cuts, -0.22, 0.18) if cuts else 1.0
    drawn = jax.random.normal(key, dims, jnp.float32) * deviation * loudness
    return jnp.minimum(jnp.maximum(drawn, -reach), reach).astype(held_as)


def setup_inputs(seed: int = 0) -> dict:
    key_of = jax.random.split(jax.random.key(seed), 13)
    hidden = normal_values(key_of[0], (TOKENS, D), 1.0, 6.0, ((0, 128),))
    w_in = normal_values(key_of[1], (D, 3 * D), D ** -0.5, 0.1875, ((0, 8),))
    conv_taps = normal_values(key_of[2], (3, D), 0.6, 3.0, (), jnp.float32)
    w_out = normal_values(key_of[3], (D, D), D ** -0.5, 0.1875, ((0, 8),))
    gain_mix = jnp.clip(1.0 + 0.18 * jax.random.normal(key_of[4], (D,), jnp.float32), 0.1, 1.9)
    gain_ffn = jnp.clip(1.0 + 0.18 * jax.random.normal(key_of[5], (D,), jnp.float32), 0.1, 1.9)
    w_gate = normal_values(key_of[6], (D, FF), D ** -0.5, 0.1875, ((0, 8),))
    w_up = normal_values(key_of[7], (D, FF), D ** -0.5, 0.1875, ((0, 8),))
    w_down = normal_values(key_of[8], (D, FF), FF ** -0.5, 0.09375, ((0, 8),))
    cotangent = normal_values(key_of[9], (TOKENS, D), 1.0, 6.0, ((0, 128),))
    counts = draw_counts(jax.random.fold_in(key_of[12], 71), 0)
    lengths = draw_lengths(jax.random.fold_in(key_of[12], 71), 0)
    return dict(hidden=hidden, w_in=w_in, conv_taps=conv_taps, w_out=w_out, gain_mix=gain_mix, gain_ffn=gain_ffn, w_gate=w_gate, w_up=w_up, w_down=w_down, cotangent=cotangent, counts=counts, lengths=lengths)


EPS = 1e-05

@jax.custom_vjp
def low(v):
    return lax.optimization_barrier(v.astype(jnp.bfloat16)).astype(jnp.float32)

@jax.custom_vjp
def low_back(v):
    return v

def low_keep(v):
    return (low(v), None)

def low_pass(kept, grad):
    return (grad,)

def back_keep(v):
    return (v, None)

def back_low(kept, grad):
    return (low(grad),)
low.defvjp(low_keep, low_pass)
low_back.defvjp(back_keep, back_low)

def matmul(left, right):
    return jnp.dot(left, right, precision=lax.Precision.HIGHEST)

def forward(stream, params, first, second):
    w_in, conv_taps, w_out, gain_mix, gain_ffn, w_gate, w_up, w_down = params
    width = stream.shape[1]
    scale_mix = lax.rsqrt(lax.optimization_barrier(jnp.mean(stream * stream, axis=1, keepdims=True)) + EPS)
    normed_mix = low(stream * scale_mix * gain_mix)
    projected = low_back(matmul(normed_mix, w_in))
    gate_b = projected[:, :width]
    gate_c = projected[:, width:2 * width]
    values = projected[:, 2 * width:]
    gated = low_back(low(gate_b * values))
    padded = jnp.concatenate([jnp.zeros((2, width), jnp.float32), gated], axis=0)
    mixed = conv_taps[2] * padded[2:] + conv_taps[1] * first * padded[1:-1] + conv_taps[0] * second * padded[:-2]
    branch_in = low(gate_c * mixed)
    attended = low_back(matmul(branch_in, w_out))
    middle = stream + attended
    scale_ffn = lax.rsqrt(lax.optimization_barrier(jnp.mean(middle * middle, axis=1, keepdims=True)) + EPS)
    normed_ffn = low(middle * scale_ffn * gain_ffn)
    gate_pre = low_back(matmul(normed_ffn, w_gate))
    up_pre = low_back(matmul(normed_ffn, w_up))
    hidden_act = low(jax.nn.silu(gate_pre) * up_pre)
    output_branch = low_back(matmul(hidden_act, w_down.T))
    return middle + output_branch

def group_step(totals, item, params):
    hidden_rows, cot_rows, group_counts, group_lengths = item
    group_rows = hidden_rows.shape[0]
    width = hidden_rows.shape[1]
    group_counts = group_counts.astype(jnp.int32)
    ends = jnp.cumsum(group_counts).astype(jnp.int32)
    offsets = (ends - group_counts).astype(jnp.int32)
    places = jnp.arange(GROUP_LIVE, dtype=jnp.int32)
    owners = lax.optimization_barrier(jnp.sum((places[:, None] >= ends[None, :]).astype(jnp.int32), axis=1)).astype(jnp.int32)
    row_ids = (owners * TOK_DEV + places - offsets[owners]).astype(jnp.int32)
    group_lengths = group_lengths.astype(jnp.int32)
    begins = (jnp.cumsum(group_lengths) - group_lengths).astype(jnp.int32)
    opens = jnp.any(places[:, None] == begins[None, :], axis=1)
    after_open = jnp.concatenate([jnp.ones((1,), jnp.bool_), opens[:-1]])
    first = jnp.where(opens, 0.0, 1.0).astype(jnp.float32)[:, None]
    second = first * jnp.where(after_open, 0.0, 1.0).astype(jnp.float32)[:, None]
    stream = hidden_rows[row_ids].astype(jnp.float32)
    cot_stream = cot_rows[row_ids].astype(jnp.float32)

    def apply_block(values, weights):
        return forward(values, weights, first, second)
    outputs, pull = jax.vjp(apply_block, stream, params)
    grad_stream, grad_params = pull(cot_stream)
    result_rows = jnp.zeros((group_rows, width), jnp.float32).at[row_ids].set(outputs)
    grad_rows = jnp.zeros((group_rows, width), jnp.float32).at[row_ids].set(grad_stream)
    new_totals = tuple((total + grad for total, grad in zip(totals, grad_params)))
    return (new_totals, (result_rows, grad_rows))

def reference(hidden, w_in, conv_taps, w_out, gain_mix, gain_ffn, w_gate, w_up, w_down, cotangent, counts, lengths):
    params = tuple((value.astype(jnp.float32) for value in (w_in, conv_taps, w_out, gain_mix, gain_ffn, w_gate, w_up, w_down)))
    width = hidden.shape[1]
    group_rows = N_SHARD * TOK_DEV
    items = (hidden.reshape(N_REP, group_rows, width), cotangent.reshape(N_REP, group_rows, width), counts, lengths)
    zeros = tuple((jnp.zeros_like(value) for value in params))
    totals, stacked = lax.scan(partial(group_step, params=params), zeros, items)
    result = stacked[0].reshape(TOKENS, width)
    grad_hidden = stacked[1].reshape(TOKENS, width)
    return (result, grad_hidden, totals[0], totals[1], totals[2], totals[3], totals[4], totals[5], totals[6], totals[7])
```

```python
import jax
import jax.numpy as jnp
from jax import lax
from jax.sharding import PartitionSpec as P

EPS = 1e-05
CONTRACT_LAST = (((1,), (1,)), ((), ()))
CONTRACT_FIRST = (((0,), (0,)), ((), ()))
AXES = ("rep", "shard")
BF16 = jnp.bfloat16
F32 = jnp.float32


def route(move):
    pairs = []
    for rep in range(16):
        for shard in range(8):
            x, y_lo = divmod(shard, 2)
            z, rest = divmod(rep, 4)
            y_hi, core = divmod(rest, 2)
            x2, y2, z2, core2 = move(x, 2 * y_hi + y_lo, z, core)
            x2, y2, z2 = x2 % 4, y2 % 4, z2 % 4
            rep2 = z2 * 4 + (y2 // 2) * 2 + core2
            pairs.append((rep * 8 + shard, rep2 * 8 + x2 * 2 + y2 % 2))
    return pairs


def send(block, dx=0, dy=0, dz=0, flip=0):
    return lax.ppermute(
        block, AXES, route(lambda x, y, z, c: (x + dx, y + dy, z + dz, c ^ flip))
    )


def send_rows(block, step):
    side = 1 if step % 2 else -1

    def move(x, y, z, core):
        if core == y % 2:
            return x + step, y, z, core
        return x + step, y + side, z, y % 2

    return lax.ppermute(block, AXES, route(move))


def dot(left, right):
    return jnp.dot(left, right, preferred_element_type=F32)


def dot_t(left, right):
    return lax.dot_general(left, right, CONTRACT_LAST, preferred_element_type=F32)


def t_dot(left, right):
    return lax.dot_general(left, right, CONTRACT_FIRST, preferred_element_type=F32)


def norm_back(grad_scaled, scaled, scale):
    return scale * (grad_scaled - scaled * jnp.mean(grad_scaled * scaled, axis=1, keepdims=True))


def pick(stack, index, axis=0):
    return lax.dynamic_index_in_dim(stack, index, axis, keepdims=False)


def in_order(parts, places, slots):
    buffer = jnp.zeros((slots,) + parts[0].shape, parts[0].dtype)
    for part, place in zip(parts, places):
        buffer = lax.dynamic_update_index_in_dim(buffer, part, place, 0)
    return buffer


class Place:
    def __init__(self):
        rep, shard = lax.axis_index("rep"), lax.axis_index("shard")
        self.shard = shard
        self.x, self.y_lo = shard // 2, shard % 2
        self.z, self.y_hi, self.core = rep // 4, (rep // 2) % 2, rep % 2
        self.y = 2 * self.y_hi + self.y_lo


def gather_z(block, at):
    parts = [block] + [send(block, dz=k) for k in (1, 3, 2)]
    return in_order(parts, [(at.z - k) % 4 for k in (0, 1, 3, 2)], 4)


def scatter_z(partial, at):
    rounded = partial.astype(BF16)
    total = pick(partial, at.z)
    parts = [send(pick(rounded, (at.z + k) % 4), dz=k) for k in (1, 3, 2)]
    for part in parts:
        total = total + part.astype(F32)
    return total


def exchange_z(block, at):
    quarter = block.shape[1] // 4
    parts = []
    for k in (0, 1, 3, 2):
        piece = lax.dynamic_slice_in_dim(block, ((at.z + k) % 4) * quarter, quarter, 1)
        parts.append(send(piece, dz=k) if k else piece)
    return in_order(parts, [(at.z - k) % 4 for k in (0, 1, 3, 2)], 4)


def gather_rows(block, at):
    steps = (0, 1, 3, 2)
    parts = [send_rows(block, k) for k in steps]
    others = [send(part, flip=1) for part in parts]
    places = [((at.x - k) % 4) * 2 + at.core for k in steps]
    places += [((at.x - k) % 4) * 2 + 1 - at.core for k in steps]
    whole = in_order(parts + others, places, 8)
    return whole.reshape(8 * block.shape[0], block.shape[1])


def columns_of(weight, at):
    width = weight.shape[1] // 4
    return lax.dynamic_slice_in_dim(weight, at.z * width, width, 1)


def sum_x(blocks, at):
    total = pick(blocks, at.x).astype(F32)
    rounded = blocks.astype(BF16)
    parts = [send(pick(rounded, (at.x + k) % 4), dx=k) for k in (1, 3, 2)]
    for part in parts:
        total = total + part.astype(F32)
    return total


def sum_y(blocks, at):
    def slot(y):
        return (y % 2) * 2 + y // 2

    total = pick(blocks, slot(at.y)).astype(F32)
    rounded = blocks.astype(BF16)
    parts = [send(pick(rounded, slot((at.y + k) % 4)), dy=k) for k in (1, 3, 2)]
    for part in parts:
        total = total + part.astype(F32)
    return total


def reduce_weights(term, at, x_first):
    columns = term.shape[1]
    cut = term.astype(BF16).reshape(4, 4, 2, 32, columns)
    got = send(pick(cut, 1 - at.core, 2), flip=1)
    half = pick(cut, at.core, 2).astype(F32) + got.astype(F32)
    if x_first:
        piece = sum_y(sum_x(half, at), at)
    else:
        piece = sum_x(sum_y(jnp.swapaxes(half, 0, 1), at), at)
    piece = piece.astype(BF16)
    slices = gather_z(piece, at)
    far = send(slices, dy=2)
    both = in_order([slices, far], [at.y_hi, 1 - at.y_hi], 2)
    twin = send(both, flip=1)
    whole = in_order([both, twin], [at.core, 1 - at.core], 2)
    return jnp.transpose(whole, (1, 0, 3, 2, 4)).reshape(128, 4, columns).astype(F32)


def sum_everywhere(rows, at):
    def ordered(parts, place):
        return jnp.sum(in_order(parts, [(place - k) % 4 for k in range(4)], 4), axis=0)

    rows = ordered([rows] + [send(rows, dx=k) for k in (1, 2, 3)], at.x)
    rows = ordered([rows] + [send(rows, dy=k) for k in (1, 2, 3)], at.y)
    rows = ordered([rows] + [send(rows, dz=k) for k in (1, 2, 3)], at.z)
    return rows + send(rows, flip=1)


def along_stream(block, distance):
    pairs = [(i, i + distance) for i in range(8) if 0 <= i + distance < 8]
    return lax.ppermute(block, "shard", pairs)


def body(
    hidden,
    w_in,
    conv_taps,
    w_out,
    gain_mix,
    gain_ffn,
    w_gate,
    w_up,
    w_down,
    cotangent,
    counts,
    lengths,
):
    height, width = hidden.shape
    quarter = width // 4
    rows = 4 * height
    at = Place()
    row_ids = jnp.arange(height, dtype=jnp.int32)
    lanes = jnp.arange(8, dtype=jnp.int32)

    own_count = jnp.sum(jnp.where(lanes == at.shard, counts[0], 0))
    own_live = (row_ids < own_count)[:, None]
    facts = gather_z(jnp.concatenate([counts, lengths], axis=1), at)[:, 0]
    all_counts, all_lengths = facts[:, :8], facts[:, 8:]
    live_rows = jnp.sum(jnp.where(lanes == at.shard, all_counts, 0), axis=1)[:, None]
    offsets = jnp.sum(jnp.where(lanes < at.shard, all_counts, 0), axis=1)[:, None]
    begins = (jnp.cumsum(all_lengths, axis=1) - all_lengths)[:, None, :]
    places = (offsets + row_ids)[:, :, None]
    first = jnp.where(jnp.any(places == begins, axis=2), 0.0, 1.0).astype(F32)
    second = first * jnp.where(jnp.any(places - 1 == begins, axis=2), 0.0, 1.0).astype(F32)
    first, second = first[:, :, None], second[:, :, None]
    ends_last = (row_ids == live_rows - 1)[:, :, None]
    ends_before = (row_ids == live_rows - 2)[:, :, None]

    out_cot = jnp.where(own_live, cotangent, jnp.zeros_like(cotangent))
    stream = gather_z(hidden, at).reshape(rows, width).astype(F32)
    mix_slice = w_in.reshape(height, 3, 4, quarter)
    mix_slice = pick(mix_slice, at.z, 2).reshape(height, 3 * quarter)
    w_mix = gather_rows(mix_slice, at)
    cot_all = gather_z(out_cot, at).reshape(rows, width)
    w_back = gather_rows(w_out, at)
    ffn_slice = jnp.concatenate([columns_of(w_gate, at), columns_of(w_up, at)], axis=1)
    w_pair = gather_rows(ffn_slice, at)
    w_low = gather_rows(columns_of(w_down, at), at)
    inner = w_low.shape[1]

    scale_mix = lax.rsqrt(jnp.mean(stream * stream, axis=1, keepdims=True) + EPS)
    scaled_mix = stream * scale_mix
    normed_mix = (scaled_mix * gain_mix).astype(BF16)
    projected = dot(normed_mix, w_mix).reshape(4, height, 3 * quarter)
    gate_b = projected[:, :, :quarter]
    gate_c = projected[:, :, quarter : 2 * quarter]
    values = projected[:, :, 2 * quarter :]
    gated = (gate_b * values).astype(BF16)
    wide = gated.astype(F32)
    tails = jnp.stack(
        [
            jnp.sum(jnp.where(ends_before, wide, 0.0), axis=1),
            jnp.sum(jnp.where(ends_last, wide, 0.0), axis=1),
        ],
        axis=1,
    ).astype(BF16)
    before = along_stream(tails, 1).astype(F32)
    taps = lax.dynamic_slice_in_dim(conv_taps, at.z * quarter, quarter, 1)
    extended = jnp.concatenate([before, wide], axis=1)
    latest = extended[:, 2:]
    previous = first * extended[:, 1:-1]
    earlier = second * extended[:, :-2]
    mixed = taps[2] * latest + taps[1] * previous + taps[0] * earlier
    branch_part = (gate_c * mixed).astype(BF16).reshape(rows, quarter)
    branch_in = gather_z(branch_part, at)
    branch_in = jnp.swapaxes(branch_in, 0, 1).reshape(rows, width)

    middle = stream + dot(branch_in, w_back)
    scale_ffn = lax.rsqrt(jnp.mean(middle * middle, axis=1, keepdims=True) + EPS)
    normed_ffn = (middle * scale_ffn * gain_ffn).astype(BF16)
    pre = dot(normed_ffn, w_pair)
    gate_pre, up_pre = pre[:, :inner], pre[:, inner:]
    sigma = jax.nn.sigmoid(gate_pre)
    silu_gate = gate_pre * sigma
    hidden_act = (silu_gate * up_pre).astype(BF16)
    grad_act = dot(cot_all, w_low)
    grad_gate = (grad_act * up_pre * (sigma * (1.0 + gate_pre * (1.0 - sigma)))).astype(BF16)
    grad_up = (grad_act * silu_gate).astype(BF16)
    grad_pair = jnp.concatenate([grad_gate, grad_up], axis=1)
    grad_normed_ffn = scatter_z(dot_t(grad_pair, w_pair).reshape(4, height, width), at)

    grad_down = reduce_weights(t_dot(cot_all, hidden_act), at, True)
    grad_pair_w = reduce_weights(t_dot(normed_ffn, grad_pair), at, False)
    output_branch = scatter_z(dot_t(hidden_act, w_low).reshape(4, height, width), at)
    own_middle = pick(middle.reshape(4, height, width), at.z)
    own_scale = pick(scale_ffn.reshape(4, height, 1), at.z)
    result = jnp.where(own_live, own_middle + output_branch, 0.0)

    own_scaled = own_middle * own_scale
    grad_gain_ffn = jnp.sum(grad_normed_ffn * own_scaled, axis=0)
    grad_middle = out_cot.astype(F32) + norm_back(
        grad_normed_ffn * gain_ffn, own_scaled, own_scale
    )
    grad_attended = grad_middle.astype(BF16)
    grad_branch = exchange_z(dot_t(grad_attended, w_back).astype(BF16), at).astype(F32)
    attended_all = gather_z(grad_attended, at).reshape(rows, width)
    grad_c = grad_branch * mixed
    grad_mixed = grad_branch * gate_c
    grad_taps = jnp.stack(
        [
            jnp.sum(grad_mixed * earlier, axis=(0, 1)),
            jnp.sum(grad_mixed * previous, axis=(0, 1)),
            jnp.sum(grad_mixed * latest, axis=(0, 1)),
        ]
    )
    grad_extended = (
        jnp.pad(taps[2] * grad_mixed, ((0, 0), (2, 0), (0, 0)))
        + jnp.pad(taps[1] * first * grad_mixed, ((0, 0), (1, 1), (0, 0)))
        + jnp.pad(taps[0] * second * grad_mixed, ((0, 0), (0, 2), (0, 0)))
    )
    returned = along_stream(grad_extended[:, :2], -1)
    grad_gated = (
        grad_extended[:, 2:]
        + jnp.where(ends_before, returned[:, :1], 0.0)
        + jnp.where(ends_last, returned[:, 1:], 0.0)
    )
    rounded_gated = grad_gated.astype(BF16).astype(F32)
    grad_projected = jnp.concatenate(
        [rounded_gated * values, grad_c, rounded_gated * gate_b], axis=2
    ).astype(BF16)
    grad_projected = grad_projected.reshape(rows, 3 * quarter)
    grad_w_in = reduce_weights(t_dot(normed_mix, grad_projected), at, True)
    part_normed_mix = dot_t(grad_projected, w_mix)
    grad_gain_mix = jnp.sum(part_normed_mix * scaled_mix, axis=0)
    grad_normed_mix = scatter_z(part_normed_mix.reshape(4, height, width), at)
    columns = lax.dynamic_slice_in_dim(attended_all, at.z * quarter, quarter, 1)
    grad_w_out = reduce_weights(t_dot(branch_in, columns), at, True)

    hidden32 = hidden.astype(F32)
    own_scale_mix = lax.rsqrt(jnp.mean(hidden32 * hidden32, axis=1, keepdims=True) + EPS)
    grad_hidden = jnp.where(
        own_live,
        grad_middle + norm_back(grad_normed_mix * gain_mix, hidden32 * own_scale_mix, own_scale_mix),
        0.0,
    )

    spread_taps = lax.dynamic_update_slice_in_dim(
        jnp.zeros((3, width), F32), grad_taps, at.z * quarter, 1
    )
    small = jnp.concatenate(
        [grad_gain_mix[None], grad_gain_ffn[None], spread_taps, jnp.zeros((3, width), F32)]
    )
    small = sum_everywhere(small, at)

    return (
        result,
        grad_hidden,
        jnp.swapaxes(grad_w_in.reshape(height, 4, 3, quarter), 1, 2).reshape(height, 3 * width),
        small[2:5],
        grad_w_out.reshape(height, width),
        small[0],
        small[1],
        grad_pair_w[:, :, :inner].reshape(height, 4 * inner),
        grad_pair_w[:, :, inner:].reshape(height, 4 * inner),
        grad_down.reshape(height, 4 * inner),
    )


def solution(mesh):
    in_specs = (
        P(("rep", "shard"), None),
        P("shard", None),
        P(),
        P("shard", None),
        P(),
        P(),
        P("shard", None),
        P("shard", None),
        P("shard", None),
        P(("rep", "shard"), None),
        P("rep", None),
        P("rep", None),
    )
    out_specs = (
        P(("rep", "shard"), None),
        P(("rep", "shard"), None),
        P("shard", None),
        P(),
        P("shard", None),
        P(),
        P(),
        P("shard", None),
        P("shard", None),
        P("shard", None),
    )
    return jax.shard_map(body, mesh=mesh, in_specs=in_specs, out_specs=out_specs, check_vma=False)
```

```python
import functools

import jax
import jax.numpy as jnp
from jax import lax
from jax.experimental import pallas as pl
from jax.experimental.pallas import tpu as pltpu
from jax.sharding import PartitionSpec as P

EPS = 1e-05
CONTRACT_LAST = (((1,), (1,)), ((), ()))
CONTRACT_FIRST = (((0,), (0,)), ((), ()))
AXES = ("rep", "shard")
BF16 = jnp.bfloat16
F32 = jnp.float32


def route(move):
    pairs = []
    for rep in range(16):
        for shard in range(8):
            x, y_lo = divmod(shard, 2)
            z, rest = divmod(rep, 4)
            y_hi, core = divmod(rest, 2)
            x2, y2, z2, core2 = move(x, 2 * y_hi + y_lo, z, core)
            x2, y2, z2 = x2 % 4, y2 % 4, z2 % 4
            rep2 = z2 * 4 + (y2 // 2) * 2 + core2
            pairs.append((rep * 8 + shard, rep2 * 8 + x2 * 2 + y2 % 2))
    return pairs


def send(block, dx=0, dy=0, dz=0, flip=0):
    return lax.ppermute(
        block, AXES, route(lambda x, y, z, c: (x + dx, y + dy, z + dz, c ^ flip))
    )


def send_rows(block, step):
    side = 1 if step % 2 else -1

    def move(x, y, z, core):
        if core == y % 2:
            return x + step, y, z, core
        return x + step, y + side, z, y % 2

    return lax.ppermute(block, AXES, route(move))


def dot(left, right):
    return jnp.dot(left, right, preferred_element_type=F32)


def dot_t(left, right):
    return lax.dot_general(left, right, CONTRACT_LAST, preferred_element_type=F32)


def t_dot(left, right):
    return lax.dot_general(left, right, CONTRACT_FIRST, preferred_element_type=F32)


def norm_back(grad_scaled, scaled, scale):
    return scale * (grad_scaled - scaled * jnp.mean(grad_scaled * scaled, axis=1, keepdims=True))


def pick(stack, index, axis=0):
    return lax.dynamic_index_in_dim(stack, index, axis, keepdims=False)


def in_order(parts, places, slots):
    buffer = jnp.zeros((slots,) + parts[0].shape, parts[0].dtype)
    for part, place in zip(parts, places):
        buffer = lax.dynamic_update_index_in_dim(buffer, part, place, 0)
    return buffer


class Place:
    def __init__(self):
        rep, shard = lax.axis_index("rep"), lax.axis_index("shard")
        self.shard = shard
        self.x, self.y_lo = shard // 2, shard % 2
        self.z, self.y_hi, self.core = rep // 4, (rep // 2) % 2, rep % 2
        self.y = 2 * self.y_hi + self.y_lo


def groups(key, order):
    found = {}
    for rep in range(16):
        for shard in range(8):
            where = (shard // 2, shard % 2, (rep // 2) % 2, rep // 4, rep % 2)
            found.setdefault(key(*where), []).append((order(*where), rep * 8 + shard))
    return [[device for _, device in sorted(members)] for members in found.values()]


ALONG_Z = groups(lambda x, yl, yh, z, c: (x, yl, yh, c), lambda x, yl, yh, z, c: z)
ROWS = groups(lambda x, yl, yh, z, c: (z, yh, c), lambda x, yl, yh, z, c: (x, yl))
OWNERS = groups(lambda x, yl, yh, z, c: (x, yl, c), lambda x, yl, yh, z, c: (yh, z))


def gather_z(block):
    whole = lax.all_gather(block, AXES, axis=0, tiled=True, axis_index_groups=ALONG_Z)
    return whole.reshape((4,) + block.shape)


def to_all(block, members):
    copies = jnp.broadcast_to(block[None], (len(members[0]),) + block.shape)
    return lax.all_to_all(copies, AXES, 0, 0, tiled=True, axis_index_groups=members)


def scatter_z(rounded, at):
    total = pick(rounded, at.z).astype(F32)
    parts = [send(pick(rounded, (at.z + k) % 4), dz=k) for k in (1, 3, 2)]
    for part in parts:
        total = total + part.astype(F32)
    return total


def by_core(mine, others, at, axis):
    return jnp.where(
        at.core == 0,
        jnp.stack([mine, others], axis=axis),
        jnp.stack([others, mine], axis=axis),
    )


STEPS = (1, 3, 2, 0)


def fetch_rows(block):
    return [send_rows(block, k) for k in STEPS]


def whole_rows(parts, at):
    half = in_order(parts, [(at.x - k) % 4 for k in STEPS], 4)
    both = by_core(half, send(half, flip=1), at, 1)
    return both.reshape(-1, half.shape[-1])


def gather_halves(block, at):
    height, columns = block.shape
    half = pick(block.reshape(2, height // 2, columns), at.core)
    half = lax.all_gather(half, AXES, axis=0, tiled=True, axis_index_groups=ROWS)
    half = half.reshape(8, height // 2, columns)
    return by_core(half, send(half, flip=1), at, 1).reshape(8 * height, columns)


def columns_of(weight, at):
    width = weight.shape[1] // 4
    return lax.dynamic_slice_in_dim(weight, at.z * width, width, 1)


def pack(rows):
    high = lax.reduce_precision(rows, 8, 7)
    return jnp.concatenate([high, rows - high]).astype(BF16)


def unpack(rows):
    rows = rows.astype(F32)
    return rows[..., :8, :] + rows[..., 8:, :]


def core_sum(term, at, small=None):
    columns = term.shape[1]
    cut = term.astype(BF16).reshape(16, 2, 32, columns)
    theirs = pick(cut, 1 - at.core, 1).reshape(512, columns)
    mine = pick(cut, at.core, 1).astype(F32)
    if small is None:
        got = send(theirs, flip=1)
        return (mine + got.reshape(16, 32, columns).astype(F32)).astype(BF16)
    packed = pack(small)
    got = send(jnp.concatenate([theirs, packed]), flip=1)
    total = (mine + got[:512].reshape(16, 32, columns).astype(F32)).astype(BF16)
    return total, unpack(packed) + unpack(got[512:])


def along_x(blocks, at, small=None):
    total = pick(blocks, at.x).astype(F32)
    return ring_sum(total, [pick(blocks, (at.x + k) % 4) for k in (1, 3, 2)], "dx", at.x, small)


def along_y(blocks, at, small=None):
    def slot(y):
        return (y % 2) * 2 + y // 2

    total = pick(blocks, slot(at.y)).astype(F32)
    pieces = [pick(blocks, slot((at.y + k) % 4)) for k in (1, 3, 2)]
    return ring_sum(total, pieces, "dy", at.y, small)


def ring_sum(total, pieces, direction, place, small):
    shape = total.shape
    count = total.size // shape[-1]
    pieces = [piece.reshape(count, shape[-1]) for piece in pieces]
    if small is not None:
        packed = pack(small)
        pieces = [jnp.concatenate([piece, packed]) for piece in pieces]
    got = [send(piece, **{direction: k}) for piece, k in zip(pieces, (1, 3, 2))]
    for part in got:
        total = total + part[:count].reshape(shape).astype(F32)
    total = total.astype(BF16)
    if small is None:
        return total
    order = [(place - k) % 4 for k in (0, 1, 3, 2)]
    smalls = in_order([packed] + [part[count:] for part in got], order, 4)
    return total, jnp.sum(unpack(smalls), axis=0)


def lay_out(layout, core_ref, mine_ref, others_ref, *out_refs):
    def write(source):
        for z in range(4):
            for start, width, out, stride, offset in layout:
                place = pl.ds(offset + z * stride, width)
                out_refs[out][:, place] = source[0, z, :32, pl.ds(start, width)].astype(F32)

    turn = pl.program_id(0) % 2
    pl.when(turn == 0)(lambda: write(mine_ref))
    pl.when(turn == 1)(lambda: write(others_ref))


def owners_rows(slices, at, layout, widths):
    others = send(slices, flip=1)
    block = (1,) + slices.shape[1:]

    def from_half(i, core):
        return (i // 2, 0, 0, 0)

    def to_row(i, core):
        return ((i // 2) * 2 + (core[0] + i) % 2, 0)

    return pl.pallas_call(
        functools.partial(lay_out, layout),
        grid_spec=pltpu.PrefetchScalarGridSpec(
            num_scalar_prefetch=1,
            grid=(4,),
            in_specs=[pl.BlockSpec(block, from_half), pl.BlockSpec(block, from_half)],
            out_specs=[pl.BlockSpec((32, width), to_row) for width in widths],
        ),
        out_shape=[jax.ShapeDtypeStruct((128, width), F32) for width in widths],
        compiler_params=pltpu.CompilerParams(vmem_limit_bytes=40 * 1024 * 1024),
    )(at.core.astype(jnp.int32).reshape(1), slices, others)


def to_partner(block):
    return lax.ppermute(block, "shard", [(i, i ^ 1) for i in range(8)])


def offer(blocks, at):
    height = blocks[0].shape[0]
    part, spare = 3 * height // 4, height // 4
    pieces = [jnp.where(at.y_lo == 0, block[part:], block[:spare]) for block in blocks]
    return to_partner(jnp.concatenate(pieces))


def even_out(blocks, got, at, first_count):
    height = blocks[0].shape[0]
    part, spare = 3 * height // 4, height // 4
    t = jnp.arange(part, dtype=jnp.int32)
    source = jnp.where(
        at.y_lo == 0,
        jnp.where(t < first_count, t, height + t - first_count),
        jnp.where(part + t < first_count, height + t, part + t - first_count),
    )
    choice = (source[:, None] == jnp.arange(height + spare, dtype=jnp.int32)).astype(BF16)
    return [
        dot(choice, jnp.concatenate([block, got[i * spare : (i + 1) * spare]])).astype(BF16)
        for i, block in enumerate(blocks)
    ]


def spread_back(block, at, first_count):
    part = block.shape[0]
    spare = part // 3
    height = part + spare
    even = at.y_lo == 0
    got = to_partner(jnp.where(even, block[part - spare :], block[:spare]))
    t = jnp.arange(height, dtype=jnp.int32)
    place = first_count + t
    source = jnp.where(
        even,
        jnp.where(t < first_count, t, -1),
        jnp.where(place >= part, place - part, spare + place),
    )
    source = jnp.where(jnp.logical_and(jnp.logical_not(even), place >= 2 * part), -1, source)
    choice = (source[:, None] == jnp.arange(height, dtype=jnp.int32)).astype(F32)
    return jnp.dot(choice, jnp.concatenate([block, got]), precision=lax.Precision.HIGHEST)


def along_stream(block, distance):
    pairs = [(i, i + distance) for i in range(8) if 0 <= i + distance < 8]
    return lax.ppermute(block, "shard", pairs)


def body(
    hidden,
    w_in,
    conv_taps,
    w_out,
    gain_mix,
    gain_ffn,
    w_gate,
    w_up,
    w_down,
    cotangent,
    counts,
    lengths,
):
    full, width = hidden.shape
    height = 3 * full // 4
    quarter = width // 4
    rows = 4 * height
    at = Place()
    lanes = jnp.arange(8, dtype=jnp.int32)
    first_count = jnp.sum(jnp.where(lanes == at.shard - at.y_lo, counts[0], 0))

    got = offer([hidden, cotangent], at)
    got, w_in, w_out, w_gate, w_up, w_down = lax.optimization_barrier(
        (got, w_in, w_out, w_gate, w_up, w_down)
    )
    own_hidden, own_cot = even_out([hidden, cotangent], got, at, first_count)
    facts = jnp.concatenate([lengths // 8, lengths % 8], axis=1).astype(BF16)
    facts = jnp.pad(facts, ((0, 15), (0, width - 8)))
    gathered = gather_z(jnp.concatenate([own_hidden, own_cot, facts]))
    stream = gathered[:, :height].reshape(rows, width).astype(F32)
    cot_all = gathered[:, height : 2 * height].reshape(rows, width)
    facts = gathered[:, 2 * height, :8].astype(F32).astype(jnp.int32)
    all_lengths = facts[:, :4] * 8 + facts[:, 4:]
    begins = (jnp.cumsum(all_lengths, axis=1) - all_lengths)[:, None, :]
    places = (at.shard * height + jnp.arange(height, dtype=jnp.int32))[None, :, None]
    first = jnp.where(jnp.any(places == begins, axis=2), 0.0, 1.0).astype(F32)
    second = first * jnp.where(jnp.any(places - 1 == begins, axis=2), 0.0, 1.0).astype(F32)
    first, second = first[:, :, None], second[:, :, None]

    mix_slice = w_in.reshape(full, 3, 4, quarter)
    mix_slice = pick(mix_slice, at.z, 2).reshape(full, 3 * quarter)
    mix_parts = fetch_rows(jnp.concatenate([mix_slice, w_out], axis=1))
    ffn_slice = jnp.concatenate([columns_of(w_gate, at), columns_of(w_up, at)], axis=1)
    mix_parts[0], ffn_slice = lax.optimization_barrier((mix_parts[0], ffn_slice))
    ffn_parts = fetch_rows(ffn_slice)
    mix_and_out = whole_rows(mix_parts, at)
    w_mix, w_back = mix_and_out[:, : 3 * quarter], mix_and_out[:, 3 * quarter :]
    w_pair = whole_rows(ffn_parts, at)
    low_slice = columns_of(w_down, at)
    inner = low_slice.shape[1]
    stream, low_slice = lax.optimization_barrier((stream, low_slice))
    w_low = gather_halves(low_slice, at)

    scale_mix = lax.rsqrt(jnp.mean(stream * stream, axis=1, keepdims=True) + EPS)
    scaled_mix = stream * scale_mix
    normed_mix = (scaled_mix * gain_mix).astype(BF16)
    projected = dot(normed_mix, w_mix).reshape(4, height, 3 * quarter)
    gate_b = projected[:, :, :quarter]
    gate_c = projected[:, :, quarter : 2 * quarter]
    values = projected[:, :, 2 * quarter :]
    gated = (gate_b * values).astype(BF16)
    before = along_stream(gated[:, height - 2 :], 1).astype(F32)
    taps = lax.dynamic_slice_in_dim(conv_taps, at.z * quarter, quarter, 1)
    extended = jnp.concatenate([before, gated.astype(F32)], axis=1)
    latest = extended[:, 2:]
    previous = first * extended[:, 1:-1]
    earlier = second * extended[:, :-2]
    mixed = taps[2] * latest + taps[1] * previous + taps[0] * earlier
    branch_part = (gate_c * mixed).astype(BF16).reshape(rows, quarter)
    branch_in = jnp.swapaxes(gather_z(branch_part), 0, 1).reshape(rows, width)

    middle = stream + dot(branch_in, w_back)
    scale_ffn = lax.rsqrt(jnp.mean(middle * middle, axis=1, keepdims=True) + EPS)
    normed_ffn = (middle * scale_ffn * gain_ffn).astype(BF16)
    pre = dot(normed_ffn, w_pair)
    gate_pre, up_pre = pre[:, :inner], pre[:, inner:]
    sigma = jax.nn.sigmoid(gate_pre)
    silu_gate = gate_pre * sigma
    hidden_act = (silu_gate * up_pre).astype(BF16)
    grad_act = dot(cot_all, w_low)
    grad_gate = (grad_act * up_pre * (sigma * (1.0 + gate_pre * (1.0 - sigma)))).astype(BF16)
    grad_up = (grad_act * silu_gate).astype(BF16)
    grad_pair = jnp.concatenate([grad_gate, grad_up], axis=1)
    part_normed_ffn = dot_t(grad_pair, w_pair).astype(BF16)
    part_normed_ffn, grad_pair, hidden_act = lax.optimization_barrier(
        (part_normed_ffn, grad_pair, hidden_act)
    )
    grad_normed_ffn = scatter_z(part_normed_ffn.reshape(4, height, width), at)
    sum_down = core_sum(t_dot(cot_all, hidden_act), at)
    sum_pair = core_sum(t_dot(normed_ffn, grad_pair), at)
    grad_normed_ffn, sum_down, sum_pair = lax.optimization_barrier(
        (grad_normed_ffn, sum_down, sum_pair)
    )
    half_down = along_x(sum_down.reshape(4, 4, 32, inner), at)
    half_pair = along_y(jnp.swapaxes(sum_pair.reshape(4, 4, 32, 2 * inner), 0, 1), at)
    own_middle = pick(middle.reshape(4, height, width), at.z)
    own_scale = pick(scale_ffn.reshape(4, height, 1), at.z)
    own_scaled = own_middle * own_scale
    grad_gain_ffn = jnp.sum(grad_normed_ffn * own_scaled, axis=0)
    grad_middle = own_cot.astype(F32) + norm_back(
        grad_normed_ffn * gain_ffn, own_scaled, own_scale
    )
    grad_attended = grad_middle.astype(BF16)
    attended_all = gather_z(grad_attended).reshape(rows, width)
    attended_all, half_down = lax.optimization_barrier((attended_all, half_down))
    output_branch = dot_t(hidden_act, w_low).astype(BF16)
    output_branch = scatter_z(output_branch.reshape(4, height, width), at)
    piece_down = along_y(half_down, at)
    piece_pair = along_x(half_pair, at)
    back_rows = lax.dynamic_slice_in_dim(w_back, at.z * quarter, quarter, 0)
    grad_branch = dot_t(attended_all, back_rows).reshape(4, height, quarter)
    grad_c = grad_branch * mixed
    grad_mixed = grad_branch * gate_c
    grad_taps = jnp.stack(
        [
            jnp.sum(grad_mixed * earlier, axis=(0, 1)),
            jnp.sum(grad_mixed * previous, axis=(0, 1)),
            jnp.sum(grad_mixed * latest, axis=(0, 1)),
        ]
    )
    grad_extended = (
        jnp.pad(taps[2] * grad_mixed, ((0, 0), (2, 0), (0, 0)))
        + jnp.pad(taps[1] * first * grad_mixed, ((0, 0), (1, 1), (0, 0)))
        + jnp.pad(taps[0] * second * grad_mixed, ((0, 0), (0, 2), (0, 0)))
    )
    returned = along_stream(grad_extended[:, :2], -1)
    grad_gated = grad_extended[:, 2:] + jnp.pad(returned, ((0, 0), (height - 2, 0), (0, 0)))
    rounded_gated = grad_gated.astype(BF16).astype(F32)
    grad_projected = jnp.concatenate(
        [rounded_gated * values, grad_c, rounded_gated * gate_b], axis=2
    ).astype(BF16)
    grad_projected = grad_projected.reshape(rows, 3 * quarter)
    part_normed_mix = dot_t(grad_projected, w_mix)
    grad_gain_mix = jnp.sum(part_normed_mix * scaled_mix, axis=0)
    columns = lax.dynamic_slice_in_dim(attended_all, at.z * quarter, quarter, 1)
    term_mix = jnp.concatenate(
        [t_dot(normed_mix, grad_projected).astype(BF16), t_dot(branch_in, columns).astype(BF16)],
        axis=1,
    )
    spread_taps = lax.dynamic_update_slice_in_dim(
        jnp.zeros((3, width), F32), grad_taps, at.z * quarter, 1
    )
    small = jnp.concatenate(
        [grad_gain_mix[None], grad_gain_ffn[None], spread_taps, jnp.zeros((3, width), F32)]
    )
    part_normed_mix = part_normed_mix.astype(BF16)
    part_normed_mix, piece_down, piece_pair, term_mix, output_branch = lax.optimization_barrier(
        (part_normed_mix, piece_down, piece_pair, term_mix, output_branch)
    )
    result = spread_back(own_middle + output_branch, at, first_count)
    slices_ffn = to_all(jnp.concatenate([piece_pair, piece_down], axis=1), OWNERS)
    slices_ffn = slices_ffn.reshape(2, 4, 32, 3 * inner)
    sum_mix, small = core_sum(term_mix, at, small)
    half_mix, small = along_x(sum_mix.reshape(4, 4, 32, width), at, small)
    piece_mix, small = along_y(half_mix, at, small)
    grad_normed_mix = scatter_z(part_normed_mix.reshape(4, height, width), at)

    hidden32 = own_hidden.astype(F32)
    own_scale_mix = lax.rsqrt(jnp.mean(hidden32 * hidden32, axis=1, keepdims=True) + EPS)
    grad_own = grad_middle + norm_back(
        grad_normed_mix * gain_mix, hidden32 * own_scale_mix, own_scale_mix
    )
    grad_hidden = spread_back(grad_own, at, first_count)

    slices_ffn, piece_mix = lax.optimization_barrier((slices_ffn, piece_mix))
    slices_mix = to_all(jnp.concatenate([piece_mix, pack(small)]), OWNERS)
    slices_mix = slices_mix.reshape(2, 4, 48, width)
    small = jnp.sum(unpack(slices_mix[0, :, 32:]), axis=0)
    layout = [(i * inner, inner, i, inner, 0) for i in range(3)]
    grad_gate, grad_up, grad_down = owners_rows(slices_ffn, at, layout, [4 * inner] * 3)
    layout = [(i * quarter, quarter, 0, quarter, i * width) for i in range(3)]
    layout.append((3 * quarter, quarter, 1, quarter, 0))
    grad_in, grad_out = owners_rows(slices_mix, at, layout, [3 * width, width])

    return (
        result,
        grad_hidden,
        grad_in,
        small[2:5],
        grad_out,
        small[0],
        small[1],
        grad_gate,
        grad_up,
        grad_down,
    )


def solution(mesh):
    in_specs = (
        P(("rep", "shard"), None),
        P("shard", None),
        P(),
        P("shard", None),
        P(),
        P(),
        P("shard", None),
        P("shard", None),
        P("shard", None),
        P(("rep", "shard"), None),
        P("rep", None),
        P("rep", None),
    )
    out_specs = (
        P(("rep", "shard"), None),
        P(("rep", "shard"), None),
        P("shard", None),
        P(),
        P("shard", None),
        P(),
        P(),
        P("shard", None),
        P("shard", None),
        P("shard", None),
    )
    return jax.shard_map(body, mesh=mesh, in_specs=in_specs, out_specs=out_specs, check_vma=False)
```

```python
import functools

import jax
import jax.numpy as jnp
from jax import lax
from jax.experimental import pallas as pl
from jax.experimental.pallas import tpu as pltpu
from jax.sharding import PartitionSpec as P

EPS = 1e-05
CONTRACT_LAST = (((1,), (1,)), ((), ()))
CONTRACT_FIRST = (((0,), (0,)), ((), ()))
AXES = ("rep", "shard")
BF16 = jnp.bfloat16
F32 = jnp.float32


def route(move):
    pairs = []
    for rep in range(16):
        for shard in range(8):
            x, y_lo = divmod(shard, 2)
            z, rest = divmod(rep, 4)
            y_hi, core = divmod(rest, 2)
            x2, y2, z2, core2 = move(x, 2 * y_hi + y_lo, z, core)
            x2, y2, z2 = x2 % 4, y2 % 4, z2 % 4
            rep2 = z2 * 4 + (y2 // 2) * 2 + core2
            pairs.append((rep * 8 + shard, rep2 * 8 + x2 * 2 + y2 % 2))
    return pairs


def send(block, dx=0, dy=0, dz=0, flip=0):
    return lax.ppermute(
        block, AXES, route(lambda x, y, z, c: (x + dx, y + dy, z + dz, c ^ flip))
    )


def send_rows(block, step):
    side = 1 if step % 2 else -1

    def move(x, y, z, core):
        if core == y % 2:
            return x + step, y, z, core
        return x + step, y + side, z, y % 2

    return lax.ppermute(block, AXES, route(move))


def dot(left, right):
    return jnp.dot(left, right, preferred_element_type=F32)


def dot_t(left, right):
    return lax.dot_general(left, right, CONTRACT_LAST, preferred_element_type=F32)


def t_dot(left, right):
    return lax.dot_general(left, right, CONTRACT_FIRST, preferred_element_type=F32)


def norm_back(grad_scaled, scaled, scale):
    return scale * (grad_scaled - scaled * jnp.mean(grad_scaled * scaled, axis=1, keepdims=True))


def pick(stack, index, axis=0):
    return lax.dynamic_index_in_dim(stack, index, axis, keepdims=False)


def in_order(parts, places, slots):
    buffer = jnp.zeros((slots,) + parts[0].shape, parts[0].dtype)
    for part, place in zip(parts, places):
        buffer = lax.dynamic_update_index_in_dim(buffer, part, place, 0)
    return buffer


class Place:
    def __init__(self):
        rep, shard = lax.axis_index("rep"), lax.axis_index("shard")
        self.shard = shard
        self.x, self.y_lo = shard // 2, shard % 2
        self.z, self.y_hi, self.core = rep // 4, (rep // 2) % 2, rep % 2
        self.y = 2 * self.y_hi + self.y_lo


def groups(key, order):
    found = {}
    for rep in range(16):
        for shard in range(8):
            where = (shard // 2, shard % 2, (rep // 2) % 2, rep // 4, rep % 2)
            found.setdefault(key(*where), []).append((order(*where), rep * 8 + shard))
    return [[device for _, device in sorted(members)] for members in found.values()]


ALONG_Z = groups(lambda x, yl, yh, z, c: (x, yl, yh, c), lambda x, yl, yh, z, c: z)
OWNERS = groups(lambda x, yl, yh, z, c: (x, yl, c), lambda x, yl, yh, z, c: (yh, z))


def gather_z(block):
    whole = lax.all_gather(block, AXES, axis=0, tiled=True, axis_index_groups=ALONG_Z)
    return whole.reshape((4,) + block.shape)


def to_all(block, members):
    copies = jnp.broadcast_to(block[None], (len(members[0]),) + block.shape)
    return lax.all_to_all(copies, AXES, 0, 0, tiled=True, axis_index_groups=members)


def scatter_z(rounded, at):
    parts = [send(pick(rounded, (at.z + k) % 4), dz=k) for k in (1, 3, 2)]
    return [pick(rounded, at.z)] + parts


def add_up(parts):
    total = parts[0].astype(F32)
    for part in parts[1:]:
        total = total + part.astype(F32)
    return total


def by_core(mine, others, at, axis):
    return jnp.where(
        at.core == 0,
        jnp.stack([mine, others], axis=axis),
        jnp.stack([others, mine], axis=axis),
    )


STEPS = (1, 3, 2, 0)


def fetch_rows(block):
    return [send_rows(block, k) for k in STEPS]


def place_rows(splits, slots_ref, *refs):
    part_refs, out_refs = refs[:8], refs[8:]

    def write(source):
        start = 0
        for width, out_ref in zip(splits, out_refs):
            out_ref[...] = source[:, pl.ds(start, width)]
            start += width

    turn = pl.program_id(0)
    for i in range(8):
        pl.when(turn == i)(functools.partial(write, part_refs[i]))


def both_cores(parts):
    return parts + [send(part, flip=1) for part in parts]


def whole_rows(parts, at, splits):
    height, columns = parts[0].shape
    slots = jnp.stack([((at.x - k) % 4) * 2 + at.core for k in STEPS])
    slots = jnp.concatenate([slots, slots + 1 - 2 * at.core]).astype(jnp.int32)
    return pl.pallas_call(
        functools.partial(place_rows, splits),
        grid_spec=pltpu.PrefetchScalarGridSpec(
            num_scalar_prefetch=1,
            grid=(8,),
            in_specs=[pl.BlockSpec((height, columns), lambda i, slots: (0, 0))] * 8,
            out_specs=[
                pl.BlockSpec((height, width), lambda i, slots: (slots[i], 0)) for width in splits
            ],
        ),
        out_shape=[jax.ShapeDtypeStruct((8 * height, width), BF16) for width in splits],
        compiler_params=pltpu.CompilerParams(vmem_limit_bytes=40 * 1024 * 1024),
    )(slots, *parts)


def columns_of(weight, at):
    width = weight.shape[1] // 4
    return lax.dynamic_slice_in_dim(weight, at.z * width, width, 1)


def pack(rows, columns):
    high = lax.reduce_precision(rows, 8, 7)
    packed = jnp.concatenate([high, rows - high]).astype(BF16)
    return jnp.pad(packed, ((0, 0), (0, columns - rows.shape[1])))


def unpack(rows):
    rows = rows.astype(F32)
    return rows[..., :8, :] + rows[..., 8:, :]


def core_sum(terms, at, small=None):
    columns = terms[0].shape[1]
    height = 32 * len(terms)
    cuts = [term.reshape(16, 2, 32, columns) for term in terms]
    theirs = jnp.concatenate([pick(cut, 1 - at.core, 1) for cut in cuts], axis=1)
    mine = jnp.concatenate([pick(cut, at.core, 1) for cut in cuts], axis=1).astype(F32)
    theirs = theirs.reshape(16 * height, columns)
    if small is not None:
        packed = pack(small, columns)
        theirs = jnp.concatenate([theirs, packed])
    got = send(theirs, flip=1)
    total = mine + got[: 16 * height].reshape(16, height, columns).astype(F32)
    if small is None:
        return total.astype(BF16)
    small = (unpack(packed) + unpack(got[16 * height :]))[:, : small.shape[1]]
    return total.astype(BF16), small


def along_x(blocks, at, small=None):
    pieces = [pick(blocks, (at.x + k) % 4) for k in (1, 3, 2)]
    return ring_sum(pick(blocks, at.x), pieces, "dx", at.x, small)


def along_y(blocks, at, small=None):
    def slot(y):
        return (y % 2) * 2 + y // 2

    pieces = [pick(blocks, slot((at.y + k) % 4)) for k in (1, 3, 2)]
    return ring_sum(pick(blocks, slot(at.y)), pieces, "dy", at.y, small)


def ring_sum(own, pieces, direction, place, small):
    count = own.shape[0]
    if small is not None:
        packed = pack(small, own.shape[1])
        pieces = [jnp.concatenate([piece, packed]) for piece in pieces]
    got = [send(piece, **{direction: k}) for piece, k in zip(pieces, (1, 3, 2))]
    total = add_up([own] + [part[:count] for part in got]).astype(BF16)
    if small is None:
        return total
    order = [(place - k) % 4 for k in (0, 1, 3, 2)]
    smalls = in_order([packed] + [part[count:] for part in got], order, 4)
    return total, jnp.sum(unpack(smalls), axis=0)[:, : small.shape[1]]


def lay_out(layout, core_ref, mine_ref, others_ref, *out_refs):
    def write(source):
        for z in range(4):
            for row, start, width, out, stride, offset in layout:
                block = source[0, z, pl.ds(row, 32), pl.ds(start, width)]
                out_refs[out][:, pl.ds(offset + z * stride, width)] = block.astype(F32)

    turn = pl.program_id(0) % 2
    pl.when(turn == 0)(lambda: write(mine_ref))
    pl.when(turn == 1)(lambda: write(others_ref))


def owners_rows(slices, at, layout, widths):
    others = send(slices, flip=1)
    block = (1,) + slices.shape[1:]

    def from_half(i, core):
        return (i // 2, 0, 0, 0)

    def to_row(i, core):
        return ((i // 2) * 2 + (core[0] + i) % 2, 0)

    return pl.pallas_call(
        functools.partial(lay_out, layout),
        grid_spec=pltpu.PrefetchScalarGridSpec(
            num_scalar_prefetch=1,
            grid=(4,),
            in_specs=[pl.BlockSpec(block, from_half), pl.BlockSpec(block, from_half)],
            out_specs=[pl.BlockSpec((32, width), to_row) for width in widths],
        ),
        out_shape=[jax.ShapeDtypeStruct((128, width), F32) for width in widths],
        compiler_params=pltpu.CompilerParams(vmem_limit_bytes=40 * 1024 * 1024),
    )(at.core.astype(jnp.int32).reshape(1), slices, others)


def to_partner(block):
    return lax.ppermute(block, "shard", [(i, i ^ 1) for i in range(8)])


def even_out(hidden, cotangent, at, counts):
    height = hidden.shape[0]
    part, spare, more = 3 * height // 4, height // 4, 3 * height // 8
    even = at.y_lo == 0
    first_count = pick(counts, at.shard - at.y_lo)
    got = to_partner(
        jnp.concatenate(
            [
                jnp.where(even, hidden[height - more :], hidden[:more]),
                jnp.where(even, cotangent[part:], cotangent[:spare]),
            ]
        )
    )

    got, hidden = lax.optimization_barrier((got, hidden))
    tail = along_stream(lax.dynamic_slice_in_dim(hidden, pick(counts, at.shard) - 2, 2), 1)

    def chosen(t, block, came, start):
        source = jnp.where(
            even,
            jnp.where(t < first_count, t, height + t - first_count),
            jnp.where(part + t < first_count, height + part + t - start, part + t - first_count),
        )
        if start < part:
            source = jnp.where(even & (t < 0), height + more + 2 + t, source)
        choice = (source[:, None] == jnp.arange(height + came.shape[0])).astype(BF16)
        return dot(choice, jnp.concatenate([block, came])).astype(BF16)

    t = jnp.arange(part, dtype=jnp.int32)
    before = jnp.arange(-2, 0, dtype=jnp.int32)
    nothing = jnp.full((height - spare // 2 - part - 2,), 4 * height, jnp.int32)
    came = jnp.concatenate([got[:more], tail, jnp.zeros((14, hidden.shape[1]), BF16)])
    rows = chosen(jnp.concatenate([t, before, nothing]), hidden, came, height - more)
    return rows, chosen(t, cotangent, got[more:], part)


def spread_back(block, at, first_count):
    part = block.shape[0]
    spare = part // 3
    height = part + spare
    even = at.y_lo == 0
    got = to_partner(jnp.where(even, block[part - spare :], block[:spare]))
    t = jnp.arange(height, dtype=jnp.int32)
    place = first_count + t
    source = jnp.where(
        even,
        jnp.where(t < first_count, t, -1),
        jnp.where(place >= part, place - part, spare + place),
    )
    source = jnp.where(jnp.logical_and(jnp.logical_not(even), place >= 2 * part), -1, source)
    choice = (source[:, None] == jnp.arange(height, dtype=jnp.int32)).astype(F32)
    return jnp.dot(choice, jnp.concatenate([block, got]), precision=lax.Precision.HIGHEST)


def along_stream(block, distance):
    pairs = [(i, i + distance) for i in range(8) if 0 <= i + distance < 8]
    return lax.ppermute(block, "shard", pairs)


def body(
    hidden,
    w_in,
    conv_taps,
    w_out,
    gain_mix,
    gain_ffn,
    w_gate,
    w_up,
    w_down,
    cotangent,
    counts,
    lengths,
):
    full, width = hidden.shape
    height = 3 * full // 4
    quarter = width // 4
    rows = 4 * height
    at = Place()
    first_count = pick(counts[0], at.shard - at.y_lo)

    own_rows, own_cot = even_out(hidden, cotangent, at, counts[0])
    own_cot, w_in, w_out = lax.optimization_barrier((own_cot, w_in, w_out))
    own_hidden = own_rows[:height]
    facts = jnp.concatenate([lengths // 8, lengths % 8], axis=1).astype(BF16)
    facts = jnp.pad(facts, ((height + 2, own_rows.shape[0] - height - 3), (0, width - 8)))
    gathered = gather_z(own_rows + facts)
    stream = gathered[:, :height].reshape(rows, width).astype(F32)

    mix_slice = w_in.reshape(full, 3, 4, quarter)
    mix_slice = pick(mix_slice, at.z, 2).reshape(full, 3 * quarter)
    mix_parts = fetch_rows(jnp.concatenate([mix_slice, w_out], axis=1))
    inner = w_down.shape[1] // 4
    ffn_slice = jnp.concatenate([columns_of(w, at) for w in (w_gate, w_up, w_down)], axis=1)
    spread_cot = jnp.pad(own_cot, ((0, full - height), (0, 0)))
    facts = gathered[:, height + 2, :8]
    facts, ffn_slice, spread_cot, *mix_parts = lax.optimization_barrier(
        (facts, ffn_slice, spread_cot, *mix_parts)
    )
    cot_all = gather_z(spread_cot)
    facts = facts.astype(F32).astype(jnp.int32)
    all_lengths = facts[:, :4] * 8 + facts[:, 4:]
    begins = (jnp.cumsum(all_lengths, axis=1) - all_lengths)[:, None, :]
    places = (at.shard * height + jnp.arange(height, dtype=jnp.int32))[None, :, None]
    first = jnp.where(jnp.any(places == begins, axis=2), 0.0, 1.0).astype(F32)
    second = first * jnp.where(jnp.any(places - 1 == begins, axis=2), 0.0, 1.0).astype(F32)
    first, second = first[:, :, None], second[:, :, None]

    ffn_parts = fetch_rows(ffn_slice)
    w_mix, w_back = whole_rows(both_cores(mix_parts), at, [3 * quarter, width])

    wide = gathered.reshape(-1, width).astype(F32)
    wide = wide * lax.rsqrt(jnp.mean(wide * wide, axis=1, keepdims=True) + EPS)
    projected = dot((wide * gain_mix).astype(BF16), w_mix).reshape(4, -1, 3 * quarter)
    gated = (projected[:, :, :quarter] * projected[:, :, 2 * quarter :]).astype(BF16)
    before = gated[:, height : height + 2].astype(F32)
    gated, projected = gated[:, :height], projected[:, :height]
    gate_b = projected[:, :, :quarter]
    gate_c = projected[:, :, quarter : 2 * quarter]
    values = projected[:, :, 2 * quarter :]
    scale_mix = lax.rsqrt(jnp.mean(stream * stream, axis=1, keepdims=True) + EPS)
    scaled_mix = stream * scale_mix
    normed_mix = (scaled_mix * gain_mix).astype(BF16)
    taps = lax.dynamic_slice_in_dim(conv_taps, at.z * quarter, quarter, 1)
    extended = jnp.concatenate([before, gated.astype(F32)], axis=1)
    latest = extended[:, 2:]
    previous = first * extended[:, 1:-1]
    earlier = second * extended[:, :-2]
    mixed = taps[2] * latest + taps[1] * previous + taps[0] * earlier
    branch_part = (gate_c * mixed).astype(BF16).reshape(rows, quarter)
    branch_in, cot_all, *ffn_parts = lax.optimization_barrier(
        (gather_z(branch_part), cot_all, *ffn_parts)
    )
    cot_all = cot_all[:, :height].reshape(rows, width)
    w_pair, w_low = whole_rows(both_cores(ffn_parts), at, [2 * inner, inner])
    branch_in = jnp.swapaxes(branch_in, 0, 1).reshape(rows, width)

    middle = stream + dot(branch_in, w_back)
    scale_ffn = lax.rsqrt(jnp.mean(middle * middle, axis=1, keepdims=True) + EPS)
    normed_ffn = (middle * scale_ffn * gain_ffn).astype(BF16)
    pre = dot(normed_ffn, w_pair)
    gate_pre, up_pre = pre[:, :inner], pre[:, inner:]
    sigma = jax.nn.sigmoid(gate_pre)
    silu_gate = gate_pre * sigma
    hidden_act = (silu_gate * up_pre).astype(BF16)
    grad_act = dot(cot_all, w_low)
    grad_gate = (grad_act * up_pre * (sigma * (1.0 + gate_pre * (1.0 - sigma)))).astype(BF16)
    grad_up = (grad_act * silu_gate).astype(BF16)
    grad_pair = jnp.concatenate([grad_gate, grad_up], axis=1)
    part_normed_ffn = dot_t(grad_pair, w_pair).astype(BF16)
    parts = scatter_z(part_normed_ffn.reshape(4, height, width), at)
    term_down = t_dot(cot_all, hidden_act).astype(BF16)
    term_pair = t_dot(normed_ffn, grad_pair).astype(BF16)
    *parts, term_down, term_pair = lax.optimization_barrier((*parts, term_down, term_pair))
    grad_normed_ffn = add_up(parts)
    sum_pair = core_sum([term_pair[:, :inner], term_pair[:, inner:]], at)
    sum_down = core_sum([term_down], at)
    half_down = along_x(sum_down.reshape(4, 128, inner), at)
    half_pair = jnp.swapaxes(sum_pair.reshape(4, 4, 64, inner), 0, 1).reshape(4, 256, inner)
    half_pair = along_y(half_pair, at)
    own_middle = pick(middle.reshape(4, height, width), at.z)
    own_scale = pick(scale_ffn.reshape(4, height, 1), at.z)
    own_scaled = own_middle * own_scale
    grad_gain_ffn = jnp.sum(grad_normed_ffn * own_scaled, axis=0)
    grad_middle = own_cot.astype(F32) + norm_back(
        grad_normed_ffn * gain_ffn, own_scaled, own_scale
    )
    grad_attended = grad_middle.astype(BF16)
    attended_all = gather_z(grad_attended).reshape(rows, width)
    attended_all, half_down, half_pair, hidden_act = lax.optimization_barrier(
        (attended_all, half_down, half_pair, hidden_act)
    )
    piece_down = along_y(half_down.reshape(4, 32, inner), at)
    piece_pair = along_x(half_pair.reshape(4, 64, inner), at)
    output_branch = lax.psum_scatter(
        dot_t(hidden_act, w_low),
        AXES,
        scatter_dimension=0,
        tiled=True,
        axis_index_groups=ALONG_Z,
    )
    back_rows = lax.dynamic_slice_in_dim(w_back, at.z * quarter, quarter, 0)
    columns = lax.dynamic_slice_in_dim(attended_all, at.z * quarter, quarter, 1)
    grad_branch = dot_t(attended_all, back_rows).reshape(4, height, quarter)
    grad_c = grad_branch * mixed
    grad_mixed = grad_branch * gate_c
    grad_taps = jnp.stack(
        [
            jnp.sum(grad_mixed * earlier, axis=(0, 1)),
            jnp.sum(grad_mixed * previous, axis=(0, 1)),
            jnp.sum(grad_mixed * latest, axis=(0, 1)),
        ]
    )
    grad_extended = (
        jnp.pad(taps[2] * grad_mixed, ((0, 0), (2, 0), (0, 0)))
        + jnp.pad(taps[1] * first * grad_mixed, ((0, 0), (1, 1), (0, 0)))
        + jnp.pad(taps[0] * second * grad_mixed, ((0, 0), (0, 2), (0, 0)))
    )
    returned = along_stream(grad_extended[:, :2], -1)
    grad_gated = grad_extended[:, 2:] + jnp.pad(returned, ((0, 0), (height - 2, 0), (0, 0)))
    rounded_gated = grad_gated.astype(BF16).astype(F32)
    grad_projected = jnp.concatenate(
        [rounded_gated * values, grad_c, rounded_gated * gate_b], axis=2
    ).astype(BF16)
    grad_projected = grad_projected.reshape(rows, 3 * quarter)
    part_normed_mix = dot_t(grad_projected, w_mix)
    grad_gain_mix = jnp.sum(part_normed_mix * scaled_mix, axis=0)
    term_mix = jnp.concatenate(
        [t_dot(normed_mix, grad_projected).astype(BF16), t_dot(branch_in, columns).astype(BF16)],
        axis=1,
    )
    spread_taps = lax.dynamic_update_slice_in_dim(
        jnp.zeros((3, width), F32), grad_taps, at.z * quarter, 1
    )
    small = jnp.concatenate(
        [grad_gain_mix[None], grad_gain_ffn[None], spread_taps, jnp.zeros((3, width), F32)]
    )
    part_normed_mix = part_normed_mix.astype(BF16)
    sum_mix, small = core_sum([term_mix], at, small)
    small, piece_down, piece_pair, output_branch = lax.optimization_barrier(
        (small, piece_down, piece_pair, output_branch)
    )
    slices_ffn = to_all(jnp.concatenate([piece_pair, piece_down]), OWNERS)
    slices_ffn = slices_ffn.reshape(2, 4, 96, inner)
    half_mix, small = along_x(sum_mix.reshape(4, 128, width), at, small)
    small, part_normed_mix = lax.optimization_barrier((small, part_normed_mix))
    piece_mix, small = along_y(half_mix.reshape(4, 32, width), at, small)
    parts = scatter_z(part_normed_mix.reshape(4, height, width), at)
    small, slices_ffn, *parts = lax.optimization_barrier((small, slices_ffn, *parts))
    grad_normed_mix = add_up(parts)
    result = spread_back(own_middle + output_branch, at, first_count)

    hidden32 = own_hidden.astype(F32)
    own_scale_mix = lax.rsqrt(jnp.mean(hidden32 * hidden32, axis=1, keepdims=True) + EPS)
    grad_own = grad_middle + norm_back(
        grad_normed_mix * gain_mix, hidden32 * own_scale_mix, own_scale_mix
    )
    grad_hidden = spread_back(grad_own, at, first_count)

    slices = to_all(jnp.concatenate([piece_mix, pack(small, width)]), OWNERS)
    slices = slices.reshape(2, 4, 48, width)
    small = jnp.sum(unpack(slices[0, :, 32:]), axis=0)
    layout = [(32 * i, 0, inner, i, inner, 0) for i in range(3)]
    grad_gate, grad_up, grad_down = owners_rows(slices_ffn, at, layout, [4 * inner] * 3)
    layout = [(0, i * quarter, quarter, 0, quarter, i * width) for i in range(3)]
    layout.append((0, 3 * quarter, quarter, 1, quarter, 0))
    grad_in, grad_out = owners_rows(slices, at, layout, [3 * width, width])

    return (
        result,
        grad_hidden,
        grad_in,
        small[2:5],
        grad_out,
        small[0],
        small[1],
        grad_gate,
        grad_up,
        grad_down,
    )


def solution(mesh):
    in_specs = (
        P(("rep", "shard"), None),
        P("shard", None),
        P(),
        P("shard", None),
        P(),
        P(),
        P("shard", None),
        P("shard", None),
        P("shard", None),
        P(("rep", "shard"), None),
        P("rep", None),
        P("rep", None),
    )
    out_specs = (
        P(("rep", "shard"), None),
        P(("rep", "shard"), None),
        P("shard", None),
        P(),
        P("shard", None),
        P(),
        P(),
        P("shard", None),
        P("shard", None),
        P("shard", None),
    )
    return jax.shard_map(body, mesh=mesh, in_specs=in_specs, out_specs=out_specs, check_vma=False)
```

```python
import functools

import jax
import jax.numpy as jnp
from jax import lax
from jax.experimental import pallas as pl
from jax.experimental.pallas import tpu as pltpu
from jax.sharding import PartitionSpec as P

EPS = 1e-05
CONTRACT_LAST = (((1,), (1,)), ((), ()))
CONTRACT_FIRST = (((0,), (0,)), ((), ()))
AXES = ("rep", "shard")
BF16 = jnp.bfloat16
F32 = jnp.float32


def route(move):
    pairs = []
    for rep in range(16):
        for shard in range(8):
            x, y_lo = divmod(shard, 2)
            z, rest = divmod(rep, 4)
            y_hi, core = divmod(rest, 2)
            x2, y2, z2, core2 = move(x, 2 * y_hi + y_lo, z, core)
            x2, y2, z2 = x2 % 4, y2 % 4, z2 % 4
            rep2 = z2 * 4 + (y2 // 2) * 2 + core2
            pairs.append((rep * 8 + shard, rep2 * 8 + x2 * 2 + y2 % 2))
    return pairs


def send(block, dx=0, dy=0, dz=0, flip=0):
    return lax.ppermute(
        block, AXES, route(lambda x, y, z, c: (x + dx, y + dy, z + dz, c ^ flip))
    )


def send_rows(block, step):
    side = 1 if step % 2 else -1

    def move(x, y, z, core):
        if core == y % 2:
            return x + step, y, z, core
        return x + step, y + side, z, y % 2

    return lax.ppermute(block, AXES, route(move))


def dot(left, right):
    return jnp.dot(left, right, preferred_element_type=F32)


def dot_t(left, right):
    return lax.dot_general(left, right, CONTRACT_LAST, preferred_element_type=F32)


def t_dot(left, right):
    return lax.dot_general(left, right, CONTRACT_FIRST, preferred_element_type=F32)


def norm_back(grad_scaled, scaled, scale):
    return scale * (grad_scaled - scaled * jnp.mean(grad_scaled * scaled, axis=1, keepdims=True))


def pick(stack, index, axis=0):
    return lax.dynamic_index_in_dim(stack, index, axis, keepdims=False)


def in_order(parts, places, slots):
    buffer = jnp.zeros((slots,) + parts[0].shape, parts[0].dtype)
    for part, place in zip(parts, places):
        buffer = lax.dynamic_update_index_in_dim(buffer, part, place, 0)
    return buffer


class Place:
    def __init__(self):
        rep, shard = lax.axis_index("rep"), lax.axis_index("shard")
        self.shard = shard
        self.x, self.y_lo = shard // 2, shard % 2
        self.z, self.y_hi, self.core = rep // 4, (rep // 2) % 2, rep % 2
        self.y = 2 * self.y_hi + self.y_lo


def groups(key, order):
    found = {}
    for rep in range(16):
        for shard in range(8):
            where = (shard // 2, shard % 2, (rep // 2) % 2, rep // 4, rep % 2)
            found.setdefault(key(*where), []).append((order(*where), rep * 8 + shard))
    return [[device for _, device in sorted(members)] for members in found.values()]


ALONG_Z = groups(lambda x, yl, yh, z, c: (x, yl, yh, c), lambda x, yl, yh, z, c: z)
OWNERS = groups(lambda x, yl, yh, z, c: (x, yl, c), lambda x, yl, yh, z, c: (yh, z))


def gather_z(block):
    whole = lax.all_gather(block, AXES, axis=0, tiled=True, axis_index_groups=ALONG_Z)
    return whole.reshape((4,) + block.shape)


def to_all(block, members):
    copies = jnp.broadcast_to(block[None], (len(members[0]),) + block.shape)
    return lax.all_to_all(copies, AXES, 0, 0, tiled=True, axis_index_groups=members)


def scatter_z(rounded, at):
    parts = [send(pick(rounded, (at.z + k) % 4), dz=k) for k in (1, 3, 2)]
    return [pick(rounded, at.z)] + parts


def add_up(parts):
    total = parts[0].astype(F32)
    for part in parts[1:]:
        total = total + part.astype(F32)
    return total


def by_core(mine, others, at, axis):
    return jnp.where(
        at.core == 0,
        jnp.stack([mine, others], axis=axis),
        jnp.stack([others, mine], axis=axis),
    )


STEPS = (1, 3, 2, 0)


def fetch_rows(block):
    return [send_rows(block, k) for k in STEPS]


def place_rows(splits, slots_ref, *refs):
    part_refs, out_refs = refs[:8], refs[8:]

    def write(source):
        start = 0
        for width, out_ref in zip(splits, out_refs):
            out_ref[...] = source[:, pl.ds(start, width)]
            start += width

    turn = pl.program_id(0)
    for i in range(8):
        pl.when(turn == i)(functools.partial(write, part_refs[i]))


def both_cores(parts):
    return parts + [send(part, flip=1) for part in parts]


def whole_rows(parts, at, splits):
    height, columns = parts[0].shape
    slots = jnp.stack([((at.x - k) % 4) * 2 + at.core for k in STEPS])
    slots = jnp.concatenate([slots, slots + 1 - 2 * at.core]).astype(jnp.int32)
    return pl.pallas_call(
        functools.partial(place_rows, splits),
        grid_spec=pltpu.PrefetchScalarGridSpec(
            num_scalar_prefetch=1,
            grid=(8,),
            in_specs=[pl.BlockSpec((height, columns), lambda i, slots: (0, 0))] * 8,
            out_specs=[
                pl.BlockSpec((height, width), lambda i, slots: (slots[i], 0)) for width in splits
            ],
        ),
        out_shape=[jax.ShapeDtypeStruct((8 * height, width), BF16) for width in splits],
        compiler_params=pltpu.CompilerParams(vmem_limit_bytes=40 * 1024 * 1024),
    )(slots, *parts)


def columns_of(weight, at):
    width = weight.shape[1] // 4
    return lax.dynamic_slice_in_dim(weight, at.z * width, width, 1)


def pack(rows, columns):
    high = lax.reduce_precision(rows, 8, 7)
    packed = jnp.concatenate([high, rows - high]).astype(BF16)
    return jnp.pad(packed, ((0, 0), (0, columns - rows.shape[1])))


def unpack(rows):
    rows = rows.astype(F32)
    return rows[..., :8, :] + rows[..., 8:, :]


def core_sum(terms, at, small=None):
    columns = terms[0].shape[1]
    height = 32 * len(terms)
    cuts = [term.reshape(16, 2, 32, columns) for term in terms]
    theirs = jnp.concatenate([pick(cut, 1 - at.core, 1) for cut in cuts], axis=1)
    mine = jnp.concatenate([pick(cut, at.core, 1) for cut in cuts], axis=1).astype(F32)
    theirs = theirs.reshape(16 * height, columns)
    if small is not None:
        packed = pack(small, columns)
        theirs = jnp.concatenate([theirs, packed])
    got = send(theirs, flip=1)
    total = mine + got[: 16 * height].reshape(16, height, columns).astype(F32)
    if small is None:
        return total.astype(BF16)
    small = (unpack(packed) + unpack(got[16 * height :]))[:, : small.shape[1]]
    return total.astype(BF16), small


def along_x(blocks, at, small=None):
    pieces = [pick(blocks, (at.x + k) % 4) for k in (1, 3, 2)]
    return ring_sum(pick(blocks, at.x), pieces, "dx", at.x, small)


def along_y(blocks, at, small=None):
    def slot(y):
        return (y % 2) * 2 + y // 2

    pieces = [pick(blocks, slot((at.y + k) % 4)) for k in (1, 3, 2)]
    return ring_sum(pick(blocks, slot(at.y)), pieces, "dy", at.y, small)


def ring_sum(own, pieces, direction, place, small):
    count = own.shape[0]
    if small is not None:
        packed = pack(small, own.shape[1])
        pieces = [jnp.concatenate([piece, packed]) for piece in pieces]
    got = [send(piece, **{direction: k}) for piece, k in zip(pieces, (1, 3, 2))]
    total = add_up([own] + [part[:count] for part in got]).astype(BF16)
    if small is None:
        return total
    order = [(place - k) % 4 for k in (0, 1, 3, 2)]
    smalls = in_order([packed] + [part[count:] for part in got], order, 4)
    return total, jnp.sum(unpack(smalls), axis=0)[:, : small.shape[1]]


def lay_out(layout, core_ref, mine_ref, others_ref, *out_refs):
    def write(source):
        for z in range(4):
            for row, start, width, out, stride, offset in layout:
                block = source[0, z, pl.ds(row, 32), pl.ds(start, width)]
                out_refs[out][:, pl.ds(offset + z * stride, width)] = block.astype(F32)

    turn = pl.program_id(0) % 2
    pl.when(turn == 0)(lambda: write(mine_ref))
    pl.when(turn == 1)(lambda: write(others_ref))


def owners_rows(slices, at, layout, widths):
    others = send(slices, flip=1)
    block = (1,) + slices.shape[1:]

    def from_half(i, core):
        return (i // 2, 0, 0, 0)

    def to_row(i, core):
        return ((i // 2) * 2 + (core[0] + i) % 2, 0)

    return pl.pallas_call(
        functools.partial(lay_out, layout),
        grid_spec=pltpu.PrefetchScalarGridSpec(
            num_scalar_prefetch=1,
            grid=(4,),
            in_specs=[pl.BlockSpec(block, from_half), pl.BlockSpec(block, from_half)],
            out_specs=[pl.BlockSpec((32, width), to_row) for width in widths],
        ),
        out_shape=[jax.ShapeDtypeStruct((128, width), F32) for width in widths],
        compiler_params=pltpu.CompilerParams(vmem_limit_bytes=40 * 1024 * 1024),
    )(at.core.astype(jnp.int32).reshape(1), slices, others)


def to_partner(block):
    return lax.ppermute(block, "shard", [(i, i ^ 1) for i in range(8)])


def even_out(hidden, cotangent, at, counts):
    height = hidden.shape[0]
    part, spare, more = 3 * height // 4, height // 4, 3 * height // 8
    even = at.y_lo == 0
    first_count = pick(counts, at.shard - at.y_lo)
    got = to_partner(
        jnp.concatenate(
            [
                jnp.where(even, hidden[height - more :], hidden[:more]),
                jnp.where(even, cotangent[part:], cotangent[:spare]),
            ]
        )
    )

    got, hidden = lax.optimization_barrier((got, hidden))
    tail = along_stream(lax.dynamic_slice_in_dim(hidden, pick(counts, at.shard) - 2, 2), 1)

    def chosen(t, block, came, start):
        source = jnp.where(
            even,
            jnp.where(t < first_count, t, height + t - first_count),
            jnp.where(part + t < first_count, height + part + t - start, part + t - first_count),
        )
        if start < part:
            source = jnp.where(even & (t < 0), height + more + 2 + t, source)
        choice = (source[:, None] == jnp.arange(height + came.shape[0])).astype(BF16)
        return dot(choice, jnp.concatenate([block, came])).astype(BF16)

    t = jnp.arange(part, dtype=jnp.int32)
    before = jnp.arange(-2, 0, dtype=jnp.int32)
    nothing = jnp.full((height - spare // 2 - part - 2,), 4 * height, jnp.int32)
    came = jnp.concatenate([got[:more], tail, jnp.zeros((14, hidden.shape[1]), BF16)])
    rows = chosen(jnp.concatenate([t, before, nothing]), hidden, came, height - more)
    return rows, chosen(t, cotangent, got[more:], part)


def spread_back(block, at, first_count):
    part = block.shape[0]
    spare = part // 3
    height = part + spare
    even = at.y_lo == 0
    got = to_partner(jnp.where(even, block[part - spare :], block[:spare]))
    t = jnp.arange(height, dtype=jnp.int32)
    place = first_count + t
    source = jnp.where(
        even,
        jnp.where(t < first_count, t, -1),
        jnp.where(place >= part, place - part, spare + place),
    )
    source = jnp.where(jnp.logical_and(jnp.logical_not(even), place >= 2 * part), -1, source)
    choice = (source[:, None] == jnp.arange(height, dtype=jnp.int32)).astype(F32)
    return jnp.dot(choice, jnp.concatenate([block, got]), precision=lax.Precision.HIGHEST)


def along_stream(block, distance):
    pairs = [(i, i + distance) for i in range(8) if 0 <= i + distance < 8]
    return lax.ppermute(block, "shard", pairs)


def body(
    hidden,
    w_in,
    conv_taps,
    w_out,
    gain_mix,
    gain_ffn,
    w_gate,
    w_up,
    w_down,
    cotangent,
    counts,
    lengths,
):
    full, width = hidden.shape
    height = 3 * full // 4
    quarter = width // 4
    rows = 4 * height
    at = Place()
    first_count = pick(counts[0], at.shard - at.y_lo)

    own_rows, own_cot = even_out(hidden, cotangent, at, counts[0])
    own_cot, w_in, w_out = lax.optimization_barrier((own_cot, w_in, w_out))
    own_hidden = own_rows[:height]
    facts = jnp.concatenate([lengths // 8, lengths % 8], axis=1).astype(BF16)
    facts = jnp.pad(facts, ((height + 2, own_rows.shape[0] - height - 3), (0, width - 8)))
    gathered = gather_z(own_rows + facts)
    stream = gathered[:, :height].reshape(rows, width).astype(F32)

    mix_slice = w_in.reshape(full, 3, 4, quarter)
    mix_slice = pick(mix_slice, at.z, 2).reshape(full, 3 * quarter)
    mix_parts = fetch_rows(jnp.concatenate([mix_slice, w_out], axis=1))
    inner = w_down.shape[1] // 4
    ffn_slice = jnp.concatenate([columns_of(w, at) for w in (w_gate, w_up, w_down)], axis=1)
    spread_cot = jnp.pad(own_cot, ((0, full - height), (0, 0)))
    facts = gathered[:, height + 2, :8]
    facts, ffn_slice, spread_cot, *mix_parts = lax.optimization_barrier(
        (facts, ffn_slice, spread_cot, *mix_parts)
    )
    cot_all = gather_z(spread_cot)
    facts = facts.astype(F32).astype(jnp.int32)
    all_lengths = facts[:, :4] * 8 + facts[:, 4:]
    begins = (jnp.cumsum(all_lengths, axis=1) - all_lengths)[:, None, :]
    places = (at.shard * height + jnp.arange(height, dtype=jnp.int32))[None, :, None]
    first = jnp.where(jnp.any(places == begins, axis=2), 0.0, 1.0).astype(F32)
    second = first * jnp.where(jnp.any(places - 1 == begins, axis=2), 0.0, 1.0).astype(F32)
    first, second = first[:, :, None], second[:, :, None]

    ffn_parts = fetch_rows(ffn_slice)
    w_mix, w_back = whole_rows(both_cores(mix_parts), at, [3 * quarter, width])

    wide = gathered.reshape(-1, width).astype(F32)
    wide = wide * lax.rsqrt(jnp.mean(wide * wide, axis=1, keepdims=True) + EPS)
    projected = dot((wide * gain_mix).astype(BF16), w_mix).reshape(4, -1, 3 * quarter)
    gated = (projected[:, :, :quarter] * projected[:, :, 2 * quarter :]).astype(BF16)
    before = gated[:, height : height + 2].astype(F32)
    gated, projected = gated[:, :height], projected[:, :height]
    gate_b = projected[:, :, :quarter]
    gate_c = projected[:, :, quarter : 2 * quarter]
    values = projected[:, :, 2 * quarter :]
    scale_mix = lax.rsqrt(jnp.mean(stream * stream, axis=1, keepdims=True) + EPS)
    scaled_mix = stream * scale_mix
    normed_mix = (scaled_mix * gain_mix).astype(BF16)
    taps = lax.dynamic_slice_in_dim(conv_taps, at.z * quarter, quarter, 1)
    extended = jnp.concatenate([before, gated.astype(F32)], axis=1)
    latest = extended[:, 2:]
    previous = first * extended[:, 1:-1]
    earlier = second * extended[:, :-2]
    mixed = taps[2] * latest + taps[1] * previous + taps[0] * earlier
    branch_part = (gate_c * mixed).astype(BF16).reshape(rows, quarter)
    branch_in, cot_all, *ffn_parts = lax.optimization_barrier(
        (gather_z(branch_part), cot_all, *ffn_parts)
    )
    cot_all = cot_all[:, :height].reshape(rows, width)
    w_pair, w_low = whole_rows(both_cores(ffn_parts), at, [2 * inner, inner])
    branch_in = jnp.swapaxes(branch_in, 0, 1).reshape(rows, width)

    middle = stream + dot(branch_in, w_back)
    scale_ffn = lax.rsqrt(jnp.mean(middle * middle, axis=1, keepdims=True) + EPS)
    normed_ffn = (middle * scale_ffn * gain_ffn).astype(BF16)
    pre = dot(normed_ffn, w_pair)
    gate_pre, up_pre = pre[:, :inner], pre[:, inner:]
    sigma = jax.nn.sigmoid(gate_pre)
    silu_gate = gate_pre * sigma
    hidden_act = (silu_gate * up_pre).astype(BF16)
    grad_act = dot(cot_all, w_low)
    grad_gate = (grad_act * up_pre * (sigma * (1.0 + gate_pre * (1.0 - sigma)))).astype(BF16)
    grad_up = (grad_act * silu_gate).astype(BF16)
    grad_pair = jnp.concatenate([grad_gate, grad_up], axis=1)
    part_normed_ffn = dot_t(grad_pair, w_pair).astype(BF16)
    parts = scatter_z(part_normed_ffn.reshape(4, height, width), at)
    term_down = t_dot(cot_all, hidden_act).astype(BF16)
    term_pair = t_dot(normed_ffn, grad_pair).astype(BF16)
    *parts, term_down, term_pair = lax.optimization_barrier((*parts, term_down, term_pair))
    grad_normed_ffn = add_up(parts)
    sum_pair = core_sum([term_pair[:, :inner], term_pair[:, inner:]], at)
    sum_down = core_sum([term_down], at)
    half_down = along_x(sum_down.reshape(4, 128, inner), at)
    half_pair = jnp.swapaxes(sum_pair.reshape(4, 4, 64, inner), 0, 1).reshape(4, 256, inner)
    half_pair = along_y(half_pair, at)
    own_middle = pick(middle.reshape(4, height, width), at.z)
    own_scale = pick(scale_ffn.reshape(4, height, 1), at.z)
    own_scaled = own_middle * own_scale
    grad_gain_ffn = jnp.sum(grad_normed_ffn * own_scaled, axis=0)
    grad_middle = own_cot.astype(F32) + norm_back(
        grad_normed_ffn * gain_ffn, own_scaled, own_scale
    )
    grad_attended = grad_middle.astype(BF16)
    attended_all = gather_z(grad_attended).reshape(rows, width)
    attended_all, half_down, hidden_act = lax.optimization_barrier(
        (attended_all, half_down, hidden_act)
    )
    piece_down = along_y(half_down.reshape(4, 32, inner), at)
    output_branch = lax.psum_scatter(
        dot_t(hidden_act, w_low),
        AXES,
        scatter_dimension=0,
        tiled=True,
        axis_index_groups=ALONG_Z,
    )
    back_rows = lax.dynamic_slice_in_dim(w_back, at.z * quarter, quarter, 0)
    columns = lax.dynamic_slice_in_dim(attended_all, at.z * quarter, quarter, 1)
    grad_branch = dot_t(attended_all, back_rows).reshape(4, height, quarter)
    grad_c = grad_branch * mixed
    grad_mixed = grad_branch * gate_c
    grad_taps = jnp.stack(
        [
            jnp.sum(grad_mixed * earlier, axis=(0, 1)),
            jnp.sum(grad_mixed * previous, axis=(0, 1)),
            jnp.sum(grad_mixed * latest, axis=(0, 1)),
        ]
    )
    grad_extended = (
        jnp.pad(taps[2] * grad_mixed, ((0, 0), (2, 0), (0, 0)))
        + jnp.pad(taps[1] * first * grad_mixed, ((0, 0), (1, 1), (0, 0)))
        + jnp.pad(taps[0] * second * grad_mixed, ((0, 0), (0, 2), (0, 0)))
    )
    returned = along_stream(grad_extended[:, :2], -1)
    grad_gated = grad_extended[:, 2:] + jnp.pad(returned, ((0, 0), (height - 2, 0), (0, 0)))
    rounded_gated = grad_gated.astype(BF16).astype(F32)
    grad_projected = jnp.concatenate(
        [rounded_gated * values, grad_c, rounded_gated * gate_b], axis=2
    ).astype(BF16)
    grad_projected = grad_projected.reshape(rows, 3 * quarter)
    grad_projected, half_pair = lax.optimization_barrier((grad_projected, half_pair))
    piece_pair = along_x(half_pair.reshape(4, 64, inner), at)
    part_normed_mix = dot_t(grad_projected, w_mix)
    grad_gain_mix = jnp.sum(part_normed_mix * scaled_mix, axis=0)
    term_mix = jnp.concatenate(
        [t_dot(normed_mix, grad_projected).astype(BF16), t_dot(branch_in, columns).astype(BF16)],
        axis=1,
    )
    spread_taps = lax.dynamic_update_slice_in_dim(
        jnp.zeros((3, width), F32), grad_taps, at.z * quarter, 1
    )
    small = jnp.concatenate(
        [grad_gain_mix[None], grad_gain_ffn[None], spread_taps, jnp.zeros((3, width), F32)]
    )
    part_normed_mix = part_normed_mix.astype(BF16)
    sum_mix, small = core_sum([term_mix], at, small)
    by_y = jnp.swapaxes(sum_mix.reshape(4, 4, 32, width), 0, 1).reshape(4, 128, width)
    half_mix, small = along_y(by_y, at, small)
    small, piece_down, piece_pair, output_branch, part_normed_mix = lax.optimization_barrier(
        (small, piece_down, piece_pair, output_branch, part_normed_mix)
    )
    slices_ffn = to_all(jnp.concatenate([piece_pair, piece_down]), OWNERS)
    slices_ffn = slices_ffn.reshape(2, 4, 96, inner)
    piece_mix, small = along_x(half_mix.reshape(4, 32, width), at, small)
    parts = scatter_z(part_normed_mix.reshape(4, height, width), at)
    small, slices_ffn, *parts = lax.optimization_barrier((small, slices_ffn, *parts))
    grad_normed_mix = add_up(parts)
    result = spread_back(own_middle + output_branch, at, first_count)

    hidden32 = own_hidden.astype(F32)
    own_scale_mix = lax.rsqrt(jnp.mean(hidden32 * hidden32, axis=1, keepdims=True) + EPS)
    grad_own = grad_middle + norm_back(
        grad_normed_mix * gain_mix, hidden32 * own_scale_mix, own_scale_mix
    )
    grad_hidden = spread_back(grad_own, at, first_count)

    slices = to_all(jnp.concatenate([piece_mix, pack(small, width)]), OWNERS)
    slices = slices.reshape(2, 4, 48, width)
    small = jnp.sum(unpack(slices[0, :, 32:]), axis=0)
    layout = [(32 * i, 0, inner, i, inner, 0) for i in range(3)]
    grad_gate, grad_up, grad_down = owners_rows(slices_ffn, at, layout, [4 * inner] * 3)
    layout = [(0, i * quarter, quarter, 0, quarter, i * width) for i in range(3)]
    layout.append((0, 3 * quarter, quarter, 1, quarter, 0))
    grad_in, grad_out = owners_rows(slices, at, layout, [3 * width, width])

    return (
        result,
        grad_hidden,
        grad_in,
        small[2:5],
        grad_out,
        small[0],
        small[1],
        grad_gate,
        grad_up,
        grad_down,
    )


def solution(mesh):
    in_specs = (
        P(("rep", "shard"), None),
        P("shard", None),
        P(),
        P("shard", None),
        P(),
        P(),
        P("shard", None),
        P("shard", None),
        P("shard", None),
        P(("rep", "shard"), None),
        P("rep", None),
        P("rep", None),
    )
    out_specs = (
        P(("rep", "shard"), None),
        P(("rep", "shard"), None),
        P("shard", None),
        P(),
        P("shard", None),
        P(),
        P(),
        P("shard", None),
        P("shard", None),
        P("shard", None),
    )
    return jax.shard_map(body, mesh=mesh, in_specs=in_specs, out_specs=out_specs, check_vma=False)
```

```python
import functools

import jax
import jax.numpy as jnp
from jax import lax
from jax.experimental import pallas as pl
from jax.experimental.pallas import tpu as pltpu
from jax.sharding import PartitionSpec as P

EPS = 1e-05
CONTRACT_LAST = (((1,), (1,)), ((), ()))
CONTRACT_FIRST = (((0,), (0,)), ((), ()))
AXES = ("rep", "shard")
BF16 = jnp.bfloat16
F32 = jnp.float32


def route(move):
    pairs = []
    for rep in range(16):
        for shard in range(8):
            x, y_lo = divmod(shard, 2)
            z, rest = divmod(rep, 4)
            y_hi, core = divmod(rest, 2)
            x2, y2, z2, core2 = move(x, 2 * y_hi + y_lo, z, core)
            x2, y2, z2 = x2 % 4, y2 % 4, z2 % 4
            rep2 = z2 * 4 + (y2 // 2) * 2 + core2
            pairs.append((rep * 8 + shard, rep2 * 8 + x2 * 2 + y2 % 2))
    return pairs


def send(block, dx=0, dy=0, dz=0, flip=0):
    return lax.ppermute(
        block, AXES, route(lambda x, y, z, c: (x + dx, y + dy, z + dz, c ^ flip))
    )


def send_rows(block, step):
    side = 1 if step % 2 else -1

    def move(x, y, z, core):
        if core == y % 2:
            return x + step, y, z, core
        return x + step, y + side, z, y % 2

    return lax.ppermute(block, AXES, route(move))


def dot(left, right):
    return jnp.dot(left, right, preferred_element_type=F32)


def dot_t(left, right):
    return lax.dot_general(left, right, CONTRACT_LAST, preferred_element_type=F32)


def t_dot(left, right):
    return lax.dot_general(left, right, CONTRACT_FIRST, preferred_element_type=F32)


def norm_back(grad_scaled, scaled, scale):
    return scale * (grad_scaled - scaled * jnp.mean(grad_scaled * scaled, axis=1, keepdims=True))


def pick(stack, index, axis=0):
    return lax.dynamic_index_in_dim(stack, index, axis, keepdims=False)


def in_order(parts, places, slots):
    buffer = jnp.zeros((slots,) + parts[0].shape, parts[0].dtype)
    for part, place in zip(parts, places):
        buffer = lax.dynamic_update_index_in_dim(buffer, part, place, 0)
    return buffer


class Place:
    def __init__(self):
        rep, shard = lax.axis_index("rep"), lax.axis_index("shard")
        self.shard = shard
        self.x, self.y_lo = shard // 2, shard % 2
        self.z, self.y_hi, self.core = rep // 4, (rep // 2) % 2, rep % 2
        self.y = 2 * self.y_hi + self.y_lo


def groups(key, order):
    found = {}
    for rep in range(16):
        for shard in range(8):
            where = (shard // 2, shard % 2, (rep // 2) % 2, rep // 4, rep % 2)
            found.setdefault(key(*where), []).append((order(*where), rep * 8 + shard))
    return [[device for _, device in sorted(members)] for members in found.values()]


ALONG_Z = groups(lambda x, yl, yh, z, c: (x, yl, yh, c), lambda x, yl, yh, z, c: z)
OWNERS = groups(lambda x, yl, yh, z, c: (x, yl, c), lambda x, yl, yh, z, c: (yh, z))


def gather_z(block):
    whole = lax.all_gather(block, AXES, axis=0, tiled=True, axis_index_groups=ALONG_Z)
    return whole.reshape((4,) + block.shape)


def to_all(block, members):
    copies = jnp.broadcast_to(block[None], (len(members[0]),) + block.shape)
    return lax.all_to_all(copies, AXES, 0, 0, tiled=True, axis_index_groups=members)


def scatter_z(rounded, at):
    parts = [send(pick(rounded, (at.z + k) % 4), dz=k) for k in (1, 3, 2)]
    return [pick(rounded, at.z)] + parts


def add_up(parts):
    total = parts[0].astype(F32)
    for part in parts[1:]:
        total = total + part.astype(F32)
    return total


def by_core(mine, others, at, axis):
    return jnp.where(
        at.core == 0,
        jnp.stack([mine, others], axis=axis),
        jnp.stack([others, mine], axis=axis),
    )


STEPS = (1, 3, 2, 0)


def fetch_rows(block):
    return [send_rows(block, k) for k in STEPS]


def place_rows(splits, slots_ref, *refs):
    part_refs, out_refs = refs[:8], refs[8:]

    def write(source):
        start = 0
        for width, out_ref in zip(splits, out_refs):
            out_ref[...] = source[:, pl.ds(start, width)]
            start += width

    turn = pl.program_id(0)
    for i in range(8):
        pl.when(turn == i)(functools.partial(write, part_refs[i]))


def both_cores(parts):
    return parts + [send(part, flip=1) for part in parts]


def whole_rows(parts, at, splits):
    height, columns = parts[0].shape
    slots = jnp.stack([((at.x - k) % 4) * 2 + at.core for k in STEPS])
    slots = jnp.concatenate([slots, slots + 1 - 2 * at.core]).astype(jnp.int32)
    return pl.pallas_call(
        functools.partial(place_rows, splits),
        grid_spec=pltpu.PrefetchScalarGridSpec(
            num_scalar_prefetch=1,
            grid=(8,),
            in_specs=[pl.BlockSpec((height, columns), lambda i, slots: (0, 0))] * 8,
            out_specs=[
                pl.BlockSpec((height, width), lambda i, slots: (slots[i], 0)) for width in splits
            ],
        ),
        out_shape=[jax.ShapeDtypeStruct((8 * height, width), BF16) for width in splits],
        compiler_params=pltpu.CompilerParams(vmem_limit_bytes=40 * 1024 * 1024),
    )(slots, *parts)


def columns_of(weight, at):
    width = weight.shape[1] // 4
    return lax.dynamic_slice_in_dim(weight, at.z * width, width, 1)


def pack(rows, columns):
    high = lax.reduce_precision(rows, 8, 7)
    packed = jnp.concatenate([high, rows - high]).astype(BF16)
    return jnp.pad(packed, ((0, 0), (0, columns - rows.shape[1])))


def unpack(rows):
    rows = rows.astype(F32)
    return rows[..., :8, :] + rows[..., 8:, :]


def core_sum(terms, at, small=None):
    columns = terms[0].shape[1]
    height = 32 * len(terms)
    cuts = [term.reshape(16, 2, 32, columns) for term in terms]
    theirs = jnp.concatenate([pick(cut, 1 - at.core, 1) for cut in cuts], axis=1)
    mine = jnp.concatenate([pick(cut, at.core, 1) for cut in cuts], axis=1).astype(F32)
    theirs = theirs.reshape(16 * height, columns)
    if small is not None:
        packed = pack(small, columns)
        theirs = jnp.concatenate([theirs, packed])
    got = send(theirs, flip=1)
    total = mine + got[: 16 * height].reshape(16, height, columns).astype(F32)
    if small is None:
        return total.astype(BF16)
    small = (unpack(packed) + unpack(got[16 * height :]))[:, : small.shape[1]]
    return total.astype(BF16), small


def along_x(blocks, at, small=None):
    pieces = [pick(blocks, (at.x + k) % 4) for k in (1, 3, 2)]
    return ring_sum(pick(blocks, at.x), pieces, "dx", at.x, small)


def along_y(blocks, at, small=None):
    def slot(y):
        return (y % 2) * 2 + y // 2

    pieces = [pick(blocks, slot((at.y + k) % 4)) for k in (1, 3, 2)]
    return ring_sum(pick(blocks, slot(at.y)), pieces, "dy", at.y, small)


def ring_sum(own, pieces, direction, place, small):
    count = own.shape[0]
    if small is not None:
        packed = pack(small, own.shape[1])
        pieces = [jnp.concatenate([piece, packed]) for piece in pieces]
    got = [send(piece, **{direction: k}) for piece, k in zip(pieces, (1, 3, 2))]
    total = add_up([own] + [part[:count] for part in got]).astype(BF16)
    if small is None:
        return total
    order = [(place - k) % 4 for k in (0, 1, 3, 2)]
    smalls = in_order([packed] + [part[count:] for part in got], order, 4)
    return total, jnp.sum(unpack(smalls), axis=0)[:, : small.shape[1]]


def lay_out(layout, core_ref, mine_ref, others_ref, *out_refs):
    def write(source):
        for z in range(4):
            for row, start, width, out, stride, offset in layout:
                block = source[0, z, pl.ds(row, 32), pl.ds(start, width)]
                out_refs[out][:, pl.ds(offset + z * stride, width)] = block.astype(F32)

    turn = pl.program_id(0) % 2
    pl.when(turn == 0)(lambda: write(mine_ref))
    pl.when(turn == 1)(lambda: write(others_ref))


def owners_rows(slices, at, layout, widths):
    others = send(slices, flip=1)
    block = (1,) + slices.shape[1:]

    def from_half(i, core):
        return (i // 2, 0, 0, 0)

    def to_row(i, core):
        return ((i // 2) * 2 + (core[0] + i) % 2, 0)

    return pl.pallas_call(
        functools.partial(lay_out, layout),
        grid_spec=pltpu.PrefetchScalarGridSpec(
            num_scalar_prefetch=1,
            grid=(4,),
            in_specs=[pl.BlockSpec(block, from_half), pl.BlockSpec(block, from_half)],
            out_specs=[pl.BlockSpec((32, width), to_row) for width in widths],
        ),
        out_shape=[jax.ShapeDtypeStruct((128, width), F32) for width in widths],
        compiler_params=pltpu.CompilerParams(vmem_limit_bytes=40 * 1024 * 1024),
    )(at.core.astype(jnp.int32).reshape(1), slices, others)


def to_partner(block):
    return lax.ppermute(block, "shard", [(i, i ^ 1) for i in range(8)])


def even_out(hidden, cotangent, at, counts):
    height = hidden.shape[0]
    part, spare, more = 3 * height // 4, height // 4, 3 * height // 8
    even = at.y_lo == 0
    first_count = pick(counts, at.shard - at.y_lo)
    got = to_partner(
        jnp.concatenate(
            [
                jnp.where(even, hidden[height - more :], hidden[:more]),
                jnp.where(even, cotangent[part:], cotangent[:spare]),
            ]
        )
    )

    got, hidden = lax.optimization_barrier((got, hidden))
    tail = along_stream(lax.dynamic_slice_in_dim(hidden, pick(counts, at.shard) - 2, 2), 1)

    def chosen(t, block, came, start):
        source = jnp.where(
            even,
            jnp.where(t < first_count, t, height + t - first_count),
            jnp.where(part + t < first_count, height + part + t - start, part + t - first_count),
        )
        if start < part:
            source = jnp.where(even & (t < 0), height + more + 2 + t, source)
        choice = (source[:, None] == jnp.arange(height + came.shape[0])).astype(BF16)
        return dot(choice, jnp.concatenate([block, came])).astype(BF16)

    t = jnp.arange(part, dtype=jnp.int32)
    before = jnp.arange(-2, 0, dtype=jnp.int32)
    nothing = jnp.full((height - spare // 2 - part - 2,), 4 * height, jnp.int32)
    came = jnp.concatenate([got[:more], tail, jnp.zeros((14, hidden.shape[1]), BF16)])
    rows = chosen(jnp.concatenate([t, before, nothing]), hidden, came, height - more)
    return rows, chosen(t, cotangent, got[more:], part)


def spread_back(block, at, first_count):
    part = block.shape[0]
    spare = part // 3
    height = part + spare
    even = at.y_lo == 0
    got = to_partner(jnp.where(even, block[part - spare :], block[:spare]))
    t = jnp.arange(height, dtype=jnp.int32)
    place = first_count + t
    source = jnp.where(
        even,
        jnp.where(t < first_count, t, -1),
        jnp.where(place >= part, place - part, spare + place),
    )
    source = jnp.where(jnp.logical_and(jnp.logical_not(even), place >= 2 * part), -1, source)
    choice = (source[:, None] == jnp.arange(height, dtype=jnp.int32)).astype(F32)
    return jnp.dot(choice, jnp.concatenate([block, got]), precision=lax.Precision.HIGHEST)


def along_stream(block, distance):
    pairs = [(i, i + distance) for i in range(8) if 0 <= i + distance < 8]
    return lax.ppermute(block, "shard", pairs)


def body(
    hidden,
    w_in,
    conv_taps,
    w_out,
    gain_mix,
    gain_ffn,
    w_gate,
    w_up,
    w_down,
    cotangent,
    counts,
    lengths,
):
    full, width = hidden.shape
    height = 3 * full // 4
    quarter = width // 4
    rows = 4 * height
    at = Place()
    first_count = pick(counts[0], at.shard - at.y_lo)

    own_rows, own_cot = even_out(hidden, cotangent, at, counts[0])
    own_cot, w_in, w_out = lax.optimization_barrier((own_cot, w_in, w_out))
    own_hidden = own_rows[:height]
    facts = jnp.concatenate([lengths // 8, lengths % 8], axis=1).astype(BF16)
    facts = jnp.pad(facts, ((height + 2, own_rows.shape[0] - height - 3), (0, width - 8)))
    gathered = gather_z(own_rows + facts)
    stream = gathered[:, :height].reshape(rows, width).astype(F32)

    mix_slice = w_in.reshape(full, 3, 4, quarter)
    mix_slice = pick(mix_slice, at.z, 2).reshape(full, 3 * quarter)
    mix_parts = fetch_rows(jnp.concatenate([mix_slice, w_out], axis=1))
    inner = w_down.shape[1] // 4
    ffn_slice = jnp.concatenate([columns_of(w, at) for w in (w_gate, w_up, w_down)], axis=1)
    spread_cot = jnp.pad(own_cot, ((0, full - height), (0, 0)))
    facts = gathered[:, height + 2, :8]
    facts, ffn_slice, spread_cot, *mix_parts = lax.optimization_barrier(
        (facts, ffn_slice, spread_cot, *mix_parts)
    )
    cot_all = gather_z(spread_cot)
    facts = facts.astype(F32).astype(jnp.int32)
    all_lengths = facts[:, :4] * 8 + facts[:, 4:]
    begins = (jnp.cumsum(all_lengths, axis=1) - all_lengths)[:, None, :]
    places = (at.shard * height + jnp.arange(height, dtype=jnp.int32))[None, :, None]
    first = jnp.where(jnp.any(places == begins, axis=2), 0.0, 1.0).astype(F32)
    second = first * jnp.where(jnp.any(places - 1 == begins, axis=2), 0.0, 1.0).astype(F32)
    first, second = first[:, :, None], second[:, :, None]

    ffn_parts = fetch_rows(ffn_slice)
    w_mix, w_back = whole_rows(both_cores(mix_parts), at, [3 * quarter, width])

    wide = gathered.reshape(-1, width).astype(F32)
    wide = wide * lax.rsqrt(jnp.mean(wide * wide, axis=1, keepdims=True) + EPS)
    projected = dot((wide * gain_mix).astype(BF16), w_mix).reshape(4, -1, 3 * quarter)
    gated = (projected[:, :, :quarter] * projected[:, :, 2 * quarter :]).astype(BF16)
    before = gated[:, height : height + 2].astype(F32)
    gated, projected = gated[:, :height], projected[:, :height]
    gate_b = projected[:, :, :quarter]
    gate_c = projected[:, :, quarter : 2 * quarter]
    values = projected[:, :, 2 * quarter :]
    scale_mix = lax.rsqrt(jnp.mean(stream * stream, axis=1, keepdims=True) + EPS)
    scaled_mix = stream * scale_mix
    normed_mix = (scaled_mix * gain_mix).astype(BF16)
    taps = lax.dynamic_slice_in_dim(conv_taps, at.z * quarter, quarter, 1)
    extended = jnp.concatenate([before, gated.astype(F32)], axis=1)
    latest = extended[:, 2:]
    previous = first * extended[:, 1:-1]
    earlier = second * extended[:, :-2]
    mixed = taps[2] * latest + taps[1] * previous + taps[0] * earlier
    branch_part = (gate_c * mixed).astype(BF16).reshape(rows, quarter)
    branch_in, cot_all, *ffn_parts = lax.optimization_barrier(
        (gather_z(branch_part), cot_all, *ffn_parts)
    )
    cot_all = cot_all[:, :height].reshape(rows, width)
    w_pair, w_low = whole_rows(both_cores(ffn_parts), at, [2 * inner, inner])
    branch_in = jnp.swapaxes(branch_in, 0, 1).reshape(rows, width)

    middle = stream + dot(branch_in, w_back)
    scale_ffn = lax.rsqrt(jnp.mean(middle * middle, axis=1, keepdims=True) + EPS)
    normed_ffn = (middle * scale_ffn * gain_ffn).astype(BF16)
    pre = dot(normed_ffn, w_pair)
    gate_pre, up_pre = pre[:, :inner], pre[:, inner:]
    sigma = jax.nn.sigmoid(gate_pre)
    silu_gate = gate_pre * sigma
    hidden_act = (silu_gate * up_pre).astype(BF16)
    grad_act = dot(cot_all, w_low)
    grad_gate = (grad_act * up_pre * (sigma * (1.0 + gate_pre * (1.0 - sigma)))).astype(BF16)
    grad_up = (grad_act * silu_gate).astype(BF16)
    grad_pair = jnp.concatenate([grad_gate, grad_up], axis=1)
    part_normed_ffn = dot_t(grad_pair, w_pair).astype(BF16)
    parts = scatter_z(part_normed_ffn.reshape(4, height, width), at)
    term_down = t_dot(cot_all, hidden_act).astype(BF16)
    term_pair = t_dot(normed_ffn, grad_pair).astype(BF16)
    *parts, term_down, term_pair = lax.optimization_barrier((*parts, term_down, term_pair))
    grad_normed_ffn = add_up(parts)
    sum_pair = core_sum([term_pair[:, :inner], term_pair[:, inner:]], at)
    sum_down = core_sum([term_down], at)
    half_down = along_x(sum_down.reshape(4, 128, inner), at)
    half_pair = jnp.swapaxes(sum_pair.reshape(4, 4, 64, inner), 0, 1).reshape(4, 256, inner)
    half_pair = along_y(half_pair, at)
    own_middle = pick(middle.reshape(4, height, width), at.z)
    own_scale = pick(scale_ffn.reshape(4, height, 1), at.z)
    own_scaled = own_middle * own_scale
    grad_gain_ffn = jnp.sum(grad_normed_ffn * own_scaled, axis=0)
    grad_middle = own_cot.astype(F32) + norm_back(
        grad_normed_ffn * gain_ffn, own_scaled, own_scale
    )
    grad_attended = grad_middle.astype(BF16)
    attended_all = gather_z(grad_attended).reshape(rows, width)
    attended_all, half_down, half_pair, hidden_act = lax.optimization_barrier(
        (attended_all, half_down, half_pair, hidden_act)
    )
    piece_down = along_y(half_down.reshape(4, 32, inner), at)
    piece_pair = along_x(half_pair.reshape(4, 64, inner), at)
    output_branch = lax.psum_scatter(
        dot_t(hidden_act, w_low),
        AXES,
        scatter_dimension=0,
        tiled=True,
        axis_index_groups=ALONG_Z,
    )
    back_rows = lax.dynamic_slice_in_dim(w_back, at.z * quarter, quarter, 0)
    columns = lax.dynamic_slice_in_dim(attended_all, at.z * quarter, quarter, 1)
    grad_branch = dot_t(attended_all, back_rows).reshape(4, height, quarter)
    grad_c = grad_branch * mixed
    grad_mixed = grad_branch * gate_c
    grad_taps = jnp.stack(
        [
            jnp.sum(grad_mixed * earlier, axis=(0, 1)),
            jnp.sum(grad_mixed * previous, axis=(0, 1)),
            jnp.sum(grad_mixed * latest, axis=(0, 1)),
        ]
    )
    grad_extended = (
        jnp.pad(taps[2] * grad_mixed, ((0, 0), (2, 0), (0, 0)))
        + jnp.pad(taps[1] * first * grad_mixed, ((0, 0), (1, 1), (0, 0)))
        + jnp.pad(taps[0] * second * grad_mixed, ((0, 0), (0, 2), (0, 0)))
    )
    returned = along_stream(grad_extended[:, :2], -1)
    grad_gated = grad_extended[:, 2:] + jnp.pad(returned, ((0, 0), (height - 2, 0), (0, 0)))
    rounded_gated = grad_gated.astype(BF16).astype(F32)
    grad_projected = jnp.concatenate(
        [rounded_gated * values, grad_c, rounded_gated * gate_b], axis=2
    ).astype(BF16)
    grad_projected = grad_projected.reshape(rows, 3 * quarter)
    part_normed_mix = dot_t(grad_projected, w_mix)
    grad_gain_mix = jnp.sum(part_normed_mix * scaled_mix, axis=0)
    term_mix = jnp.concatenate(
        [t_dot(normed_mix, grad_projected).astype(BF16), t_dot(branch_in, columns).astype(BF16)],
        axis=1,
    )
    spread_taps = lax.dynamic_update_slice_in_dim(
        jnp.zeros((3, width), F32), grad_taps, at.z * quarter, 1
    )
    small = jnp.concatenate(
        [grad_gain_mix[None], grad_gain_ffn[None], spread_taps, jnp.zeros((3, width), F32)]
    )
    part_normed_mix = part_normed_mix.astype(BF16)
    sum_mix, small = core_sum([term_mix], at, small)
    small, piece_down, piece_pair, output_branch = lax.optimization_barrier(
        (small, piece_down, piece_pair, output_branch)
    )
    by_y = jnp.swapaxes(sum_mix.reshape(4, 4, 32, width), 0, 1).reshape(4, 128, width)
    half_mix, small = along_y(by_y, at, small)
    piece_ffn = jnp.concatenate([piece_pair, piece_down])
    small, piece_ffn, part_normed_mix = lax.optimization_barrier(
        (small, piece_ffn, part_normed_mix)
    )
    slices_ffn = to_all(piece_ffn, OWNERS).reshape(2, 4, 96, inner)
    piece_mix, small = along_x(half_mix.reshape(4, 32, width), at, small)
    parts = scatter_z(part_normed_mix.reshape(4, height, width), at)
    small, slices_ffn, *parts = lax.optimization_barrier((small, slices_ffn, *parts))
    grad_normed_mix = add_up(parts)
    result = spread_back(own_middle + output_branch, at, first_count)

    hidden32 = own_hidden.astype(F32)
    own_scale_mix = lax.rsqrt(jnp.mean(hidden32 * hidden32, axis=1, keepdims=True) + EPS)
    grad_own = grad_middle + norm_back(
        grad_normed_mix * gain_mix, hidden32 * own_scale_mix, own_scale_mix
    )
    grad_hidden = spread_back(grad_own, at, first_count)

    slices = to_all(jnp.concatenate([piece_mix, pack(small, width)]), OWNERS)
    slices = slices.reshape(2, 4, 48, width)
    layout = [(32 * i, 0, inner, i, inner, 0) for i in range(3)]
    grad_gate, grad_up, grad_down = owners_rows(slices_ffn, at, layout, [4 * inner] * 3)
    slices, grad_gate, grad_up, grad_down = lax.optimization_barrier(
        (slices, grad_gate, grad_up, grad_down)
    )
    layout = [(0, i * quarter, quarter, 0, quarter, i * width) for i in range(3)]
    layout.append((0, 3 * quarter, quarter, 1, quarter, 0))
    small = jnp.sum(unpack(slices[0, :, 32:]), axis=0)
    grad_in, grad_out = owners_rows(slices, at, layout, [3 * width, width])

    return (
        result,
        grad_hidden,
        grad_in,
        small[2:5],
        grad_out,
        small[0],
        small[1],
        grad_gate,
        grad_up,
        grad_down,
    )


def solution(mesh):
    in_specs = (
        P(("rep", "shard"), None),
        P("shard", None),
        P(),
        P("shard", None),
        P(),
        P(),
        P("shard", None),
        P("shard", None),
        P("shard", None),
        P(("rep", "shard"), None),
        P("rep", None),
        P("rep", None),
    )
    out_specs = (
        P(("rep", "shard"), None),
        P(("rep", "shard"), None),
        P("shard", None),
        P(),
        P("shard", None),
        P(),
        P(),
        P("shard", None),
        P("shard", None),
        P("shard", None),
    )
    return jax.shard_map(body, mesh=mesh, in_specs=in_specs, out_specs=out_specs, check_vma=False)
```

```python
import functools

import jax
import jax.numpy as jnp
from jax import lax
from jax.experimental import pallas as pl
from jax.experimental.pallas import tpu as pltpu
from jax.sharding import PartitionSpec as P

EPS = 1e-05
CONTRACT_LAST = (((1,), (1,)), ((), ()))
CONTRACT_FIRST = (((0,), (0,)), ((), ()))
AXES = ("rep", "shard")
BF16 = jnp.bfloat16
F32 = jnp.float32


def route(move):
    pairs = []
    for rep in range(16):
        for shard in range(8):
            x, y_lo = divmod(shard, 2)
            z, rest = divmod(rep, 4)
            y_hi, core = divmod(rest, 2)
            x2, y2, z2, core2 = move(x, 2 * y_hi + y_lo, z, core)
            x2, y2, z2 = x2 % 4, y2 % 4, z2 % 4
            rep2 = z2 * 4 + (y2 // 2) * 2 + core2
            pairs.append((rep * 8 + shard, rep2 * 8 + x2 * 2 + y2 % 2))
    return pairs


def send(block, dx=0, dy=0, dz=0, flip=0):
    return lax.ppermute(
        block, AXES, route(lambda x, y, z, c: (x + dx, y + dy, z + dz, c ^ flip))
    )


def send_rows(block, step):
    side = 1 if step % 2 else -1

    def move(x, y, z, core):
        if core == y % 2:
            return x + step, y, z, core
        return x + step, y + side, z, y % 2

    return lax.ppermute(block, AXES, route(move))


def dot(left, right):
    return jnp.dot(left, right, preferred_element_type=F32)


def dot_t(left, right):
    return lax.dot_general(left, right, CONTRACT_LAST, preferred_element_type=F32)


def t_dot(left, right):
    return lax.dot_general(left, right, CONTRACT_FIRST, preferred_element_type=F32)


def norm_back(grad_scaled, scaled, scale):
    return scale * (grad_scaled - scaled * jnp.mean(grad_scaled * scaled, axis=1, keepdims=True))


def pick(stack, index, axis=0):
    return lax.dynamic_index_in_dim(stack, index, axis, keepdims=False)


def in_order(parts, places, slots):
    buffer = jnp.zeros((slots,) + parts[0].shape, parts[0].dtype)
    for part, place in zip(parts, places):
        buffer = lax.dynamic_update_index_in_dim(buffer, part, place, 0)
    return buffer


class Place:
    def __init__(self):
        rep, shard = lax.axis_index("rep"), lax.axis_index("shard")
        self.shard = shard
        self.x, self.y_lo = shard // 2, shard % 2
        self.z, self.y_hi, self.core = rep // 4, (rep // 2) % 2, rep % 2
        self.y = 2 * self.y_hi + self.y_lo


def groups(key, order):
    found = {}
    for rep in range(16):
        for shard in range(8):
            where = (shard // 2, shard % 2, (rep // 2) % 2, rep // 4, rep % 2)
            found.setdefault(key(*where), []).append((order(*where), rep * 8 + shard))
    return [[device for _, device in sorted(members)] for members in found.values()]


ALONG_Z = groups(lambda x, yl, yh, z, c: (x, yl, yh, c), lambda x, yl, yh, z, c: z)
ROWS = groups(lambda x, yl, yh, z, c: (z, yh, c), lambda x, yl, yh, z, c: (x, yl))
OWNERS = groups(lambda x, yl, yh, z, c: (x, yl, c), lambda x, yl, yh, z, c: (yh, z))


def gather_z(block):
    whole = lax.all_gather(block, AXES, axis=0, tiled=True, axis_index_groups=ALONG_Z)
    return whole.reshape((4,) + block.shape)


def to_all(block, members):
    copies = jnp.broadcast_to(block[None], (len(members[0]),) + block.shape)
    return lax.all_to_all(copies, AXES, 0, 0, tiled=True, axis_index_groups=members)


def scatter_z(rounded, at):
    total = pick(rounded, at.z).astype(F32)
    parts = [send(pick(rounded, (at.z + k) % 4), dz=k) for k in (1, 3, 2)]
    for part in parts:
        total = total + part.astype(F32)
    return total


def by_core(mine, others, at, axis):
    return jnp.where(
        at.core == 0,
        jnp.stack([mine, others], axis=axis),
        jnp.stack([others, mine], axis=axis),
    )


STEPS = (1, 3, 2, 0)


def fetch_rows(block):
    return [send_rows(block, k) for k in STEPS]


def whole_rows(parts, at):
    half = in_order(parts, [(at.x - k) % 4 for k in STEPS], 4)
    both = by_core(half, send(half, flip=1), at, 1)
    return both.reshape(-1, half.shape[-1])


def gather_halves(block, at):
    height, columns = block.shape
    half = pick(block.reshape(2, height // 2, columns), at.core)
    half = lax.all_gather(half, AXES, axis=0, tiled=True, axis_index_groups=ROWS)
    half = half.reshape(8, height // 2, columns)
    return by_core(half, send(half, flip=1), at, 1).reshape(8 * height, columns)


def columns_of(weight, at):
    width = weight.shape[1] // 4
    return lax.dynamic_slice_in_dim(weight, at.z * width, width, 1)


def pack(rows):
    high = lax.reduce_precision(rows, 8, 7)
    return jnp.concatenate([high, rows - high]).astype(BF16)


def unpack(rows):
    rows = rows.astype(F32)
    return rows[..., :8, :] + rows[..., 8:, :]


def core_sum(term, at, small=None):
    columns = term.shape[1]
    cut = term.astype(BF16).reshape(16, 2, 32, columns)
    theirs = pick(cut, 1 - at.core, 1).reshape(512, columns)
    mine = pick(cut, at.core, 1).astype(F32)
    if small is None:
        got = send(theirs, flip=1)
        return (mine + got.reshape(16, 32, columns).astype(F32)).astype(BF16)
    packed = pack(small)
    got = send(jnp.concatenate([theirs, packed]), flip=1)
    total = (mine + got[:512].reshape(16, 32, columns).astype(F32)).astype(BF16)
    return total, unpack(packed) + unpack(got[512:])


def along_x(blocks, at, small=None):
    total = pick(blocks, at.x).astype(F32)
    return ring_sum(total, [pick(blocks, (at.x + k) % 4) for k in (1, 3, 2)], "dx", at.x, small)


def along_y(blocks, at, small=None):
    def slot(y):
        return (y % 2) * 2 + y // 2

    total = pick(blocks, slot(at.y)).astype(F32)
    pieces = [pick(blocks, slot((at.y + k) % 4)) for k in (1, 3, 2)]
    return ring_sum(total, pieces, "dy", at.y, small)


def ring_sum(total, pieces, direction, place, small):
    shape = total.shape
    count = total.size // shape[-1]
    pieces = [piece.reshape(count, shape[-1]) for piece in pieces]
    if small is not None:
        packed = pack(small)
        pieces = [jnp.concatenate([piece, packed]) for piece in pieces]
    got = [send(piece, **{direction: k}) for piece, k in zip(pieces, (1, 3, 2))]
    for part in got:
        total = total + part[:count].reshape(shape).astype(F32)
    total = total.astype(BF16)
    if small is None:
        return total
    order = [(place - k) % 4 for k in (0, 1, 3, 2)]
    smalls = in_order([packed] + [part[count:] for part in got], order, 4)
    return total, jnp.sum(unpack(smalls), axis=0)


def lay_out(layout, core_ref, mine_ref, others_ref, *out_refs):
    def write(source):
        for z in range(4):
            for start, width, out, stride, offset in layout:
                place = pl.ds(offset + z * stride, width)
                out_refs[out][:, place] = source[0, z, :32, pl.ds(start, width)].astype(F32)

    turn = pl.program_id(0) % 2
    pl.when(turn == 0)(lambda: write(mine_ref))
    pl.when(turn == 1)(lambda: write(others_ref))


def owners_rows(slices, at, layout, widths):
    others = send(slices, flip=1)
    block = (1,) + slices.shape[1:]

    def from_half(i, core):
        return (i // 2, 0, 0, 0)

    def to_row(i, core):
        return ((i // 2) * 2 + (core[0] + i) % 2, 0)

    return pl.pallas_call(
        functools.partial(lay_out, layout),
        grid_spec=pltpu.PrefetchScalarGridSpec(
            num_scalar_prefetch=1,
            grid=(4,),
            in_specs=[pl.BlockSpec(block, from_half), pl.BlockSpec(block, from_half)],
            out_specs=[pl.BlockSpec((32, width), to_row) for width in widths],
        ),
        out_shape=[jax.ShapeDtypeStruct((128, width), F32) for width in widths],
        compiler_params=pltpu.CompilerParams(vmem_limit_bytes=40 * 1024 * 1024),
    )(at.core.astype(jnp.int32).reshape(1), slices, others)


def to_partner(block):
    return lax.ppermute(block, "shard", [(i, i ^ 1) for i in range(8)])


def offer(blocks, at):
    height = blocks[0].shape[0]
    part, spare = 3 * height // 4, height // 4
    pieces = [jnp.where(at.y_lo == 0, block[part:], block[:spare]) for block in blocks]
    return to_partner(jnp.concatenate(pieces))


def even_out(blocks, got, at, first_count):
    height = blocks[0].shape[0]
    part, spare = 3 * height // 4, height // 4
    t = jnp.arange(part, dtype=jnp.int32)
    source = jnp.where(
        at.y_lo == 0,
        jnp.where(t < first_count, t, height + t - first_count),
        jnp.where(part + t < first_count, height + t, part + t - first_count),
    )
    choice = (source[:, None] == jnp.arange(height + spare, dtype=jnp.int32)).astype(BF16)
    return [
        dot(choice, jnp.concatenate([block, got[i * spare : (i + 1) * spare]])).astype(BF16)
        for i, block in enumerate(blocks)
    ]


def spread_back(block, at, first_count):
    part = block.shape[0]
    spare = part // 3
    height = part + spare
    even = at.y_lo == 0
    got = to_partner(jnp.where(even, block[part - spare :], block[:spare]))
    t = jnp.arange(height, dtype=jnp.int32)
    place = first_count + t
    source = jnp.where(
        even,
        jnp.where(t < first_count, t, -1),
        jnp.where(place >= part, place - part, spare + place),
    )
    source = jnp.where(jnp.logical_and(jnp.logical_not(even), place >= 2 * part), -1, source)
    choice = (source[:, None] == jnp.arange(height, dtype=jnp.int32)).astype(F32)
    return jnp.dot(choice, jnp.concatenate([block, got]), precision=lax.Precision.HIGHEST)


def along_stream(block, distance):
    pairs = [(i, i + distance) for i in range(8) if 0 <= i + distance < 8]
    return lax.ppermute(block, "shard", pairs)


def body(
    hidden,
    w_in,
    conv_taps,
    w_out,
    gain_mix,
    gain_ffn,
    w_gate,
    w_up,
    w_down,
    cotangent,
    counts,
    lengths,
):
    full, width = hidden.shape
    height = 3 * full // 4
    quarter = width // 4
    rows = 4 * height
    at = Place()
    lanes = jnp.arange(8, dtype=jnp.int32)
    first_count = jnp.sum(jnp.where(lanes == at.shard - at.y_lo, counts[0], 0))

    got = offer([hidden, cotangent], at)
    got, w_in, w_out, w_gate, w_up, w_down = lax.optimization_barrier(
        (got, w_in, w_out, w_gate, w_up, w_down)
    )
    own_hidden, own_cot = even_out([hidden, cotangent], got, at, first_count)
    facts = jnp.concatenate([lengths // 8, lengths % 8], axis=1).astype(BF16)
    facts = jnp.pad(facts, ((0, 15), (0, width - 8)))
    gathered = gather_z(jnp.concatenate([own_hidden, own_cot, facts]))
    stream = gathered[:, :height].reshape(rows, width).astype(F32)
    cot_all = gathered[:, height : 2 * height].reshape(rows, width)
    facts = gathered[:, 2 * height, :8].astype(F32).astype(jnp.int32)
    all_lengths = facts[:, :4] * 8 + facts[:, 4:]
    begins = (jnp.cumsum(all_lengths, axis=1) - all_lengths)[:, None, :]
    places = (at.shard * height + jnp.arange(height, dtype=jnp.int32))[None, :, None]
    first = jnp.where(jnp.any(places == begins, axis=2), 0.0, 1.0).astype(F32)
    second = first * jnp.where(jnp.any(places - 1 == begins, axis=2), 0.0, 1.0).astype(F32)
    first, second = first[:, :, None], second[:, :, None]

    mix_slice = w_in.reshape(full, 3, 4, quarter)
    mix_slice = pick(mix_slice, at.z, 2).reshape(full, 3 * quarter)
    mix_parts = fetch_rows(jnp.concatenate([mix_slice, w_out], axis=1))
    ffn_slice = jnp.concatenate([columns_of(w_gate, at), columns_of(w_up, at)], axis=1)
    mix_parts[0], ffn_slice = lax.optimization_barrier((mix_parts[0], ffn_slice))
    ffn_parts = fetch_rows(ffn_slice)
    mix_and_out = whole_rows(mix_parts, at)
    w_mix, w_back = mix_and_out[:, : 3 * quarter], mix_and_out[:, 3 * quarter :]
    w_pair = whole_rows(ffn_parts, at)
    low_slice = columns_of(w_down, at)
    inner = low_slice.shape[1]
    stream, low_slice = lax.optimization_barrier((stream, low_slice))
    w_low = gather_halves(low_slice, at)

    scale_mix = lax.rsqrt(jnp.mean(stream * stream, axis=1, keepdims=True) + EPS)
    scaled_mix = stream * scale_mix
    normed_mix = (scaled_mix * gain_mix).astype(BF16)
    projected = dot(normed_mix, w_mix).reshape(4, height, 3 * quarter)
    gate_b = projected[:, :, :quarter]
    gate_c = projected[:, :, quarter : 2 * quarter]
    values = projected[:, :, 2 * quarter :]
    gated = (gate_b * values).astype(BF16)
    before = along_stream(gated[:, height - 2 :], 1).astype(F32)
    taps = lax.dynamic_slice_in_dim(conv_taps, at.z * quarter, quarter, 1)
    extended = jnp.concatenate([before, gated.astype(F32)], axis=1)
    latest = extended[:, 2:]
    previous = first * extended[:, 1:-1]
    earlier = second * extended[:, :-2]
    mixed = taps[2] * latest + taps[1] * previous + taps[0] * earlier
    branch_part = (gate_c * mixed).astype(BF16).reshape(rows, quarter)
    branch_in = jnp.swapaxes(gather_z(branch_part), 0, 1).reshape(rows, width)

    middle = stream + dot(branch_in, w_back)
    scale_ffn = lax.rsqrt(jnp.mean(middle * middle, axis=1, keepdims=True) + EPS)
    normed_ffn = (middle * scale_ffn * gain_ffn).astype(BF16)
    pre = dot(normed_ffn, w_pair)
    gate_pre, up_pre = pre[:, :inner], pre[:, inner:]
    sigma = jax.nn.sigmoid(gate_pre)
    silu_gate = gate_pre * sigma
    hidden_act = (silu_gate * up_pre).astype(BF16)
    grad_act = dot(cot_all, w_low)
    grad_gate = (grad_act * up_pre * (sigma * (1.0 + gate_pre * (1.0 - sigma)))).astype(BF16)
    grad_up = (grad_act * silu_gate).astype(BF16)
    grad_pair = jnp.concatenate([grad_gate, grad_up], axis=1)
    part_normed_ffn = dot_t(grad_pair, w_pair).astype(BF16)
    part_normed_ffn, grad_pair, hidden_act = lax.optimization_barrier(
        (part_normed_ffn, grad_pair, hidden_act)
    )
    grad_normed_ffn = scatter_z(part_normed_ffn.reshape(4, height, width), at)
    sum_down = core_sum(t_dot(cot_all, hidden_act), at)
    sum_pair = core_sum(t_dot(normed_ffn, grad_pair), at)
    grad_normed_ffn, sum_down, sum_pair = lax.optimization_barrier(
        (grad_normed_ffn, sum_down, sum_pair)
    )
    half_down = along_x(sum_down.reshape(4, 4, 32, inner), at)
    half_pair = along_y(jnp.swapaxes(sum_pair.reshape(4, 4, 32, 2 * inner), 0, 1), at)
    own_middle = pick(middle.reshape(4, height, width), at.z)
    own_scale = pick(scale_ffn.reshape(4, height, 1), at.z)
    own_scaled = own_middle * own_scale
    grad_gain_ffn = jnp.sum(grad_normed_ffn * own_scaled, axis=0)
    grad_middle = own_cot.astype(F32) + norm_back(
        grad_normed_ffn * gain_ffn, own_scaled, own_scale
    )
    grad_attended = grad_middle.astype(BF16)
    attended_all = gather_z(grad_attended).reshape(rows, width)
    attended_all, half_down = lax.optimization_barrier((attended_all, half_down))
    output_branch = dot_t(hidden_act, w_low).astype(BF16)
    output_branch = scatter_z(output_branch.reshape(4, height, width), at)
    piece_down = along_y(half_down, at)
    piece_pair = along_x(half_pair, at)
    back_rows = lax.dynamic_slice_in_dim(w_back, at.z * quarter, quarter, 0)
    grad_branch = dot_t(attended_all, back_rows).reshape(4, height, quarter)
    grad_c = grad_branch * mixed
    grad_mixed = grad_branch * gate_c
    grad_taps = jnp.stack(
        [
            jnp.sum(grad_mixed * earlier, axis=(0, 1)),
            jnp.sum(grad_mixed * previous, axis=(0, 1)),
            jnp.sum(grad_mixed * latest, axis=(0, 1)),
        ]
    )
    grad_extended = (
        jnp.pad(taps[2] * grad_mixed, ((0, 0), (2, 0), (0, 0)))
        + jnp.pad(taps[1] * first * grad_mixed, ((0, 0), (1, 1), (0, 0)))
        + jnp.pad(taps[0] * second * grad_mixed, ((0, 0), (0, 2), (0, 0)))
    )
    returned = along_stream(grad_extended[:, :2], -1)
    grad_gated = grad_extended[:, 2:] + jnp.pad(returned, ((0, 0), (height - 2, 0), (0, 0)))
    rounded_gated = grad_gated.astype(BF16).astype(F32)
    grad_projected = jnp.concatenate(
        [rounded_gated * values, grad_c, rounded_gated * gate_b], axis=2
    ).astype(BF16)
    grad_projected = grad_projected.reshape(rows, 3 * quarter)
    part_normed_mix = dot_t(grad_projected, w_mix)
    grad_gain_mix = jnp.sum(part_normed_mix * scaled_mix, axis=0)
    columns = lax.dynamic_slice_in_dim(attended_all, at.z * quarter, quarter, 1)
    term_mix = jnp.concatenate(
        [t_dot(normed_mix, grad_projected).astype(BF16), t_dot(branch_in, columns).astype(BF16)],
        axis=1,
    )
    spread_taps = lax.dynamic_update_slice_in_dim(
        jnp.zeros((3, width), F32), grad_taps, at.z * quarter, 1
    )
    small = jnp.concatenate(
        [grad_gain_mix[None], grad_gain_ffn[None], spread_taps, jnp.zeros((3, width), F32)]
    )
    part_normed_mix = part_normed_mix.astype(BF16)
    part_normed_mix, piece_down, piece_pair, term_mix, output_branch = lax.optimization_barrier(
        (part_normed_mix, piece_down, piece_pair, term_mix, output_branch)
    )
    result = spread_back(own_middle + output_branch, at, first_count)
    slices_ffn = to_all(jnp.concatenate([piece_pair, piece_down], axis=1), OWNERS)
    slices_ffn = slices_ffn.reshape(2, 4, 32, 3 * inner)
    sum_mix, small = core_sum(term_mix, at, small)
    half_mix, small = along_x(sum_mix.reshape(4, 4, 32, width), at, small)
    small, part_normed_mix = lax.optimization_barrier((small, part_normed_mix))
    piece_mix, small = along_y(half_mix, at, small)
    grad_normed_mix = scatter_z(part_normed_mix.reshape(4, height, width), at)

    hidden32 = own_hidden.astype(F32)
    own_scale_mix = lax.rsqrt(jnp.mean(hidden32 * hidden32, axis=1, keepdims=True) + EPS)
    grad_own = grad_middle + norm_back(
        grad_normed_mix * gain_mix, hidden32 * own_scale_mix, own_scale_mix
    )
    grad_hidden = spread_back(grad_own, at, first_count)

    slices_ffn, piece_mix = lax.optimization_barrier((slices_ffn, piece_mix))
    slices_mix = to_all(jnp.concatenate([piece_mix, pack(small)]), OWNERS)
    slices_mix = slices_mix.reshape(2, 4, 48, width)
    small = jnp.sum(unpack(slices_mix[0, :, 32:]), axis=0)
    layout = [(i * inner, inner, i, inner, 0) for i in range(3)]
    grad_gate, grad_up, grad_down = owners_rows(slices_ffn, at, layout, [4 * inner] * 3)
    slices_mix, grad_gate, grad_up, grad_down = lax.optimization_barrier(
        (slices_mix, grad_gate, grad_up, grad_down)
    )
    layout = [(i * quarter, quarter, 0, quarter, i * width) for i in range(3)]
    layout.append((3 * quarter, quarter, 1, quarter, 0))
    grad_in, grad_out = owners_rows(slices_mix, at, layout, [3 * width, width])

    return (
        result,
        grad_hidden,
        grad_in,
        small[2:5],
        grad_out,
        small[0],
        small[1],
        grad_gate,
        grad_up,
        grad_down,
    )


def solution(mesh):
    in_specs = (
        P(("rep", "shard"), None),
        P("shard", None),
        P(),
        P("shard", None),
        P(),
        P(),
        P("shard", None),
        P("shard", None),
        P("shard", None),
        P(("rep", "shard"), None),
        P("rep", None),
        P("rep", None),
    )
    out_specs = (
        P(("rep", "shard"), None),
        P(("rep", "shard"), None),
        P("shard", None),
        P(),
        P("shard", None),
        P(),
        P(),
        P("shard", None),
        P("shard", None),
        P("shard", None),
    )
    return jax.shard_map(body, mesh=mesh, in_specs=in_specs, out_specs=out_specs, check_vma=False)
```
